32 devices in a mesh: seq: 4 (over y, x), dp: 8 (over z, core).
Axes of the slice: x: 2, y: 2, z: 4, core: 2. Of those that a mesh axis runs over, the one named last changes fastest.
Arguments:
- inputs: bfloat16 [24, 2048, 768], P('dp', 'seq'), may hold values from -6 to 6
- cotangent: bfloat16 [24, 2048, 768], P('dp', 'seq'), may hold values from -24 to 24
- lengths: int32 [24], P('dp'), may hold values from 1 to 2048, as said below
- triple_weight: bfloat16 [768, 2304], replicated, may hold values from -0.21875 to 0.21875
- output_weight: bfloat16 [768, 768], replicated, may hold values from -6 to 6
- inner_weight: bfloat16 [768, 3072], replicated, may hold values from -0.21875 to 0.21875
- outer_weight: bfloat16 [3072, 768], replicated, may hold values from -0.109375 to 0.109375
- attn_gain: float32 [768], replicated, may hold values from 0.25 to 1.75
- ffn_gain: float32 [768], replicated, may hold values from 0.25 to 1.75
- query_bias: float32 [768], replicated, may hold values from -1.5 to 1.5
- value_bias: float32 [768], replicated, may hold values from -0.1 to 0.1
- output_bias: float32 [768], replicated, may hold values from -1.5 to 1.5
- attn_shift: float32 [768], replicated, may hold values from -1.5 to 1.5
- inner_bias: float32 [3072], replicated, may hold values from -1.5 to 1.5
- outer_bias: float32 [768], replicated, may hold values from -1.5 to 1.5
- ffn_shift: float32 [768], replicated, may hold values from -1.5 to 1.5
Outputs:
- layer_out: bfloat16 [24, 2048, 768], P('dp', 'seq')
- input_grad: bfloat16 [24, 2048, 768], P('dp', 'seq')
- query_bias_grad: float32 [768], replicated
- value_bias_grad: float32 [768], replicated
- output_bias_grad: float32 [768], replicated
- attn_shift_grad: float32 [768], replicated
- inner_bias_grad: float32 [3072], replicated
- outer_bias_grad: float32 [768], replicated
- ffn_shift_grad: float32 [768], replicated
The draws below stay inside these ranges and needn't reach their ends.
Inputs may be any that keep to these rules, and one draw needn't show every extreme that they name: `lengths`: among the 3 sequences that one index of dp holds, at least one has length 2048.
All inputs are finite; a program needn't handle non-finite values.
Results may differ from the reference program's by a relative error of at most 0.017.
Values may be sent and summed in bfloat16 or wider, within the bound.
No kernel may reach another device: no remote copies, remote signals or barrier semaphores. Data moves between devices by JAX's collectives and lax.ppermute only.
A program may use at most 320 MiB of HBM per device.

```python
import math
import jax
import jax.numpy as jnp
from jax import lax

D = 768
HEADS = 12
HEAD = 64
FF = 3072
LEN = 2048
SEQ_DEV = 3
SEQS = 24


def draw_lengths(key, part):
    key = jax.random.fold_in(key, 5)
    first_key, second_key = jax.random.split(key)
    drawn = jax.random.randint(first_key, (SEQS // SEQ_DEV, SEQ_DEV), 1, LEN + 1, dtype=jnp.int32)
    chosen = jax.random.randint(second_key, (SEQS // SEQ_DEV, 1), 0, SEQ_DEV, dtype=jnp.int32)
    slots = jnp.arange(SEQ_DEV, dtype=jnp.int32)[None, :]
    return jnp.where(slots == chosen, LEN, drawn).reshape(SEQS).astype(jnp.int32)


def draw_cotangent(key, part):
    key = jax.random.fold_in(key, 9)
    noise_key = jax.random.fold_in(key, 0)
    noise = jnp.clip(jax.random.normal(noise_key, (SEQS, LEN, D), jnp.float32), -5.0, 5.0)
    seq_place = (jnp.arange(SEQS, dtype=jnp.float32) / (SEQS - 1))[:, None, None]
    tok_place = (jnp.arange(LEN, dtype=jnp.float32) / (LEN - 1))[None, :, None]
    rising = (1.0 + 2.0 * seq_place) * (1.0 + 2.0 * tok_place) / 3.0
    return (rising * noise).astype(jnp.bfloat16)


def levels(key, extent, pieces, least, largest):
    factor_of, own = 1.0, jax.random.fold_in(key, 6)
    for axis_at, parts in pieces:
        draws = jnp.exp(jax.random.uniform(jax.random.fold_in(own, axis_at), (parts,), jnp.float32, least / len(pieces), largest / len(pieces)))
        factor_of = factor_of * jnp.repeat(draws, extent[axis_at] // parts).reshape([-1 if axis == axis_at else 1 for axis in range(len(extent))])
    return factor_of


def normal_values(own_key, extent, scale, reach, cuts=(), held_as=jnp.bfloat16):
    level = levels(own_key, extent, cuts, -0.22, 0.18) if cuts else 1.0
    values = jax.random.normal(own_key, extent, jnp.float32) * scale * level
    return jnp.minimum(jnp.maximum(values, -reach), reach).astype(held_as)


def setup_inputs(seed: int = 0) -> dict:
    seeds = jax.random.split(jax.random.key(seed), 17)
    return {
        "inputs": normal_values(seeds[0], (SEQS, LEN, D), 1.0, 6.0, ((0, 8), (1, 4))),
        "cotangent": draw_cotangent(jax.random.fold_in(seeds[16], 71), 0),
        "lengths": draw_lengths(jax.random.fold_in(seeds[16], 71), 0),
        "triple_weight": normal_values(seeds[3], (D, 3 * D), D ** -0.5, 0.21875),
        "output_weight": normal_values(seeds[4], (D, D), (max(4 * D // LEN, 1)) ** -0.5, 6.0),
        "inner_weight": normal_values(seeds[5], (D, FF), D ** -0.5, 0.21875),
        "outer_weight": normal_values(seeds[6], (FF, D), FF ** -0.5, 0.109375),
        "attn_gain": jnp.clip(1.0 + 0.15 * jax.random.normal(seeds[7], (D,), jnp.float32), 0.25, 1.75),
        "ffn_gain": jnp.clip(1.0 + 0.15 * jax.random.normal(seeds[8], (D,), jnp.float32), 0.25, 1.75),
        "query_bias": normal_values(seeds[9], (D,), 0.3, 1.5, (), jnp.float32),
        "value_bias": normal_values(seeds[10], (D,), 0.02, 0.1, (), jnp.float32),
        "output_bias": normal_values(seeds[11], (D,), 0.3, 1.5, (), jnp.float32),
        "attn_shift": normal_values(seeds[12], (D,), 0.3, 1.5, (), jnp.float32),
        "inner_bias": normal_values(seeds[13], (FF,), 0.3, 1.5, (), jnp.float32),
        "outer_bias": normal_values(seeds[14], (D,), 0.3, 1.5, (), jnp.float32),
        "ffn_shift": normal_values(seeds[15], (D,), 0.3, 1.5, (), jnp.float32),
    }


@jax.custom_vjp
def low(v):
    return lax.optimization_barrier(v.astype(jnp.bfloat16)).astype(jnp.float32)

@jax.custom_vjp
def low_back(v):
    return v

def low_keep(v):
    return (low(v), None)

def low_pass(kept, grad):
    return (grad,)

def back_keep(v):
    return (v, None)

def back_low(kept, grad):
    return (low(grad),)
low.defvjp(low_keep, low_pass)
low_back.defvjp(back_keep, back_low)
epsilon = 1e-06
floor_score = -1e+30
highest = lax.Precision.HIGHEST

def product(left, right):
    return jnp.dot(left, right, precision=highest)

def normalize(hidden, gain, shift):
    center = hidden - lax.optimization_barrier(jnp.mean(hidden, -1, keepdims=True))
    variance = lax.optimization_barrier(jnp.mean(center * center, -1, keepdims=True))
    return center * lax.rsqrt(variance + epsilon) * gain + shift

def attend(queries, key_rows, value_rows, length):
    split = (LEN, HEADS, HEAD)
    scaling = 1.0 / math.sqrt(HEAD)
    scores = jnp.einsum('qhd,khd->qhk', queries.reshape(split), key_rows.reshape(split), precision=highest) * scaling
    usable = jnp.arange(LEN, dtype=jnp.int32) < length
    scores = low_back(jnp.where(usable[None, None, :], scores, floor_score))
    shifted = jnp.exp(scores - lax.optimization_barrier(jnp.max(scores, -1, keepdims=True)))
    probs = shifted / lax.optimization_barrier(jnp.sum(shifted, -1, keepdims=True))
    mixed = jnp.einsum('qhk,khd->qhd', low(probs), value_rows.reshape(split), precision=highest)
    return low(low_back(mixed.reshape(LEN, D)))

def layer(sequence, length, frozen, biases):
    triple_weight, output_weight, inner_weight, outer_weight, attn_gain, ffn_gain = frozen
    query_bias, value_bias, output_bias, attn_shift, inner_bias, outer_bias, ffn_shift = biases
    projection = product(sequence, triple_weight)
    queries = low(low_back(projection[:, :D]) + query_bias)
    key_rows = low(low_back(projection[:, D:2 * D]))
    value_rows = low(low_back(projection[:, 2 * D:]) + value_bias)
    context = jax.checkpoint(attend)(queries, key_rows, value_rows, length)
    middle = normalize(sequence + low_back(product(context, output_weight)) + output_bias, attn_gain, attn_shift)
    hidden = low_back(product(low(middle), inner_weight)) + inner_bias
    projected = low_back(product(low(jax.nn.gelu(hidden, approximate=False)), outer_weight)) + outer_bias
    return normalize(middle + projected, ffn_gain, ffn_shift)

def reference(inputs, cotangent, lengths, triple_weight, output_weight, inner_weight, outer_weight, attn_gain, ffn_gain, query_bias, value_bias, output_bias, attn_shift, inner_bias, outer_bias, ffn_shift):
    frozen = tuple((tensor.astype(jnp.float32) for tensor in (triple_weight, output_weight, inner_weight, outer_weight, attn_gain, ffn_gain)))
    biases = tuple((tensor.astype(jnp.float32) for tensor in (query_bias, value_bias, output_bias, attn_shift, inner_bias, outer_bias, ffn_shift)))

    def visit_one(running, scan_item):
        sequence, grad_out, length = scan_item

        def run_layer(seq_in, bias_in):
            return layer(seq_in, length, frozen, bias_in)
        result, pullback = jax.vjp(run_layer, sequence.astype(jnp.float32), biases)
        seq_grad, bias_grads = pullback(grad_out.astype(jnp.float32))
        running = tuple((earlier + later for earlier, later in zip(running, bias_grads)))
        return (running, (result.astype(jnp.bfloat16), seq_grad.astype(jnp.bfloat16)))
    initial = tuple((jnp.zeros_like(tensor) for tensor in biases))
    totals, outputs = lax.scan(visit_one, initial, (inputs, cotangent, lengths))
    layer_out, input_grad = outputs
    return (layer_out, input_grad, totals[0], totals[1], totals[2], totals[3], totals[4], totals[5], totals[6])
```

```python
import functools
import math

import jax
import jax.numpy as jnp
from jax import lax
from jax.experimental import pallas as pl
from jax.experimental.pallas import tpu as pltpu
from jax.sharding import PartitionSpec as P

HEAD = 64
PAIR = 128
epsilon = 1e-06
NEG = -1e30
SUM_LOW, SUM_HIGH = 2.0**-90, 2.0**100
bf16, f32 = jnp.bfloat16, jnp.float32
VMEM = 56 << 20


def nn(a, b):
    return lax.dot_general(a, b, (((1,), (0,)), ((), ())), preferred_element_type=f32)


def nt(a, b):
    return lax.dot_general(a, b, (((1,), (1,)), ((), ())), preferred_element_type=f32)


def split3(value):
    first = value.astype(bf16).astype(f32)
    second = (value - first).astype(bf16).astype(f32)
    return first, second, value - first - second


def sizes(keys):
    return max(keys // 2, 128), max(keys // 4, 128)


def over_keys(length, keys, step):
    big, small = sizes(keys)
    count = (length + small - 1) // small
    ratio = big // small
    full = count // ratio

    def turn(i, carried):
        step(pl.multiple_of(i * big, big), big)
        return carried

    lax.fori_loop(0, full, turn, 0)
    if ratio > 1:

        @pl.when(count > full * ratio)
        def _():
            step(pl.multiple_of(full * big, small), small)


def pipelined(units, first, second):
    held = None
    for unit in units:
        result = first(unit)
        if held is not None:
            second(*held)
        held = (unit, result)
    second(*held)


def in_head(index, h):
    return (index >= HEAD) == (h == 1)


def forward_kernel(length_ref, q_ref, k_ref, v_ref, p_ref, ctx_ref, linv_ref, acc_ref, top_ref):
    length = length_ref[0]
    rows, keys = q_ref.shape[0], k_ref.shape[0]
    part = min(rows, 256)
    lane = lax.broadcasted_iota(jnp.int32, (rows, PAIR), 1)

    def queries(h, top):
        other = HEAD * (1 - h)
        a, b, c = split3(-top)
        extra = jnp.where(lane == other + 3, 1.0, 0.0)
        for j, piece in enumerate((a, b, c)):
            extra = jnp.where(lane == other + j, piece, extra)
        return jnp.where(in_head(lane, h), q_ref[...].astype(f32), extra).astype(bf16)

    def key_side(h, start, size):
        other = HEAD * (1 - h)
        at = lax.broadcasted_iota(jnp.int32, (size, PAIR), 1)
        place = start + lax.broadcasted_iota(jnp.int32, (size, PAIR), 0)
        extra = jnp.where(at == other + 3, jnp.where(place < length, 0.0, NEG), 1.0).astype(bf16)
        return jnp.where(in_head(at, h), k_ref[pl.ds(start, size)], extra).T

    def sweep(sides):
        acc_ref[...] = jnp.zeros_like(acc_ref)

        def step(start, size):
            at = lax.broadcasted_iota(jnp.int32, (size, PAIR), 1)
            values = v_ref[pl.ds(start, size)]
            one = jnp.ones((), bf16)
            kt = [key_side(h, start, size) for h in range(2)]
            va = [jnp.where(in_head(at, h), values, one) for h in range(2)]

            def score(unit):
                h, c = unit
                return nn(sides[h][c : c + part], kt[h])

            def weigh(unit, s):
                h, c = unit
                p = jnp.exp2(s).astype(bf16)
                p_ref[h, c : c + part, pl.ds(start, size)] = p
                acc_ref[h, c : c + part] += nn(p, va[h])

            pipelined([(h, c) for h in range(2) for c in range(0, rows, part)], score, weigh)

        over_keys(length, keys, step)

    zero = jnp.zeros((rows, 1), f32)
    plain = [queries(h, zero) for h in range(2)]
    sweep(plain)

    def sums():
        return jnp.where(lane < HEAD, acc_ref[1], acc_ref[0])

    total = sums()
    fine = jnp.logical_and(jnp.min(total) > SUM_LOW, jnp.max(total) < SUM_HIGH)

    @pl.when(jnp.logical_not(fine))
    def _():
        top_ref[...] = jnp.full_like(top_ref, NEG)

        def step(start, size):
            for h in range(2):
                s = nn(plain[h], key_side(h, start, size))
                top_ref[h] = jnp.maximum(top_ref[h], jnp.max(s, 1, keepdims=True))

        over_keys(length, keys, step)
        sweep([queries(h, top_ref[h][:, :1]) for h in range(2)])

    inverse = pltpu.roll(1.0 / sums(), HEAD, 1)
    linv_ref[...] = inverse
    ctx_ref[...] = (jnp.where(lane < HEAD, acc_ref[0], acc_ref[1]) * inverse).astype(bf16)


def attention_forward(length, queries, key_rows, value_rows):
    rows, width = queries.shape
    keys = key_rows.shape[0]
    pairs = width // PAIR
    qspec = pl.BlockSpec((rows, PAIR), lambda p, n: (0, p))
    kspec = pl.BlockSpec((keys, PAIR), lambda p, n: (0, p))
    return pl.pallas_call(
        forward_kernel,
        grid_spec=pltpu.PrefetchScalarGridSpec(
            num_scalar_prefetch=1,
            grid=(pairs,),
            in_specs=[qspec, kspec, kspec],
            out_specs=[pl.BlockSpec((2, rows, keys), lambda p, n: (p, 0, 0)), qspec, qspec],
            scratch_shapes=[pltpu.VMEM((2, rows, PAIR), f32), pltpu.VMEM((2, rows, PAIR), f32)],
        ),
        out_shape=[
            jax.ShapeDtypeStruct((2 * pairs, rows, keys), bf16),
            jax.ShapeDtypeStruct((rows, width), bf16),
            jax.ShapeDtypeStruct((rows, width), f32),
        ],
        compiler_params=pltpu.CompilerParams(vmem_limit_bytes=VMEM),
        cost_estimate=pl.CostEstimate(
            flops=16 * rows * keys * width, bytes_accessed=2 * rows * keys * width // HEAD, transcendentals=0
        ),
        name="attention_forward",
    )(length, queries, key_rows, value_rows)


def backward_kernel(
    length_ref, q_ref, g_ref, ctx_ref, linv_ref, k_ref, v_ref, p_ref,
    dq_ref, dk_ref, dv_ref, acc_ref, dkt_ref, dvt_ref,
):
    length = length_ref[0]
    rows, keys = q_ref.shape[0], k_ref.shape[0]
    lane = lax.broadcasted_iota(jnp.int32, (rows, PAIR), 1)
    grad = g_ref[...].astype(f32)
    inverse = linv_ref[...]
    product = grad * ctx_ref[...].astype(f32) * inverse
    scaled = grad * inverse
    sides = []
    for h in range(2):
        other = HEAD * (1 - h)
        delta = jnp.sum(jnp.where(in_head(lane, h), product, 0.0), 1, keepdims=True)
        extra = jnp.zeros((rows, PAIR), f32)
        for j, piece in enumerate(split3(-delta)):
            extra = jnp.where(lane == other + j, piece, extra)
        sides.append(jnp.where(in_head(lane, h), scaled, extra).astype(bf16))
    gt = scaled.astype(bf16).T
    qt = q_ref[...].T
    acc_ref[...] = jnp.zeros_like(acc_ref)
    big, small = sizes(keys)
    count = (length + small - 1) // small

    def step(start, size):
        at = lax.broadcasted_iota(jnp.int32, (size, PAIR), 1)
        span = pl.ds(start, size)
        key_rows, value_rows = k_ref[span], v_ref[span]
        one = jnp.ones((), bf16)
        vt = [jnp.where(in_head(at, h), value_rows, one).T for h in range(2)]

        def first(h):
            return nn(sides[h], vt[h])

        def second(h, dp):
            p = p_ref[h, :, span]
            ds = (p.astype(f32) * dp).astype(bf16)
            acc_ref[h] += nn(ds, key_rows)
            mine = slice(HEAD * h, HEAD * h + HEAD)
            dvt_ref[mine, :size] = nn(gt, p)[mine]
            dkt_ref[mine, :size] = nn(qt, ds)[mine]

        pipelined(range(2), first, second)
        dk_ref[span] = (dkt_ref[:, :size] * math.log(2.0)).astype(bf16).T
        dv_ref[span] = dvt_ref[:, :size].astype(bf16).T

    over_keys(length, keys, step)

    def blank(i, carried):
        span = pl.ds(pl.multiple_of(i * small, small), small)
        dk_ref[span] = jnp.zeros((small, PAIR), bf16)
        dv_ref[span] = jnp.zeros((small, PAIR), bf16)
        return carried

    lax.fori_loop(count, keys // small, blank, 0)
    dq_ref[...] = jnp.where(lane < HEAD, acc_ref[0], acc_ref[1]) * (1.0 / math.sqrt(HEAD))


def attention_backward(length, queries, grads, context, linv, key_rows, value_rows, weights):
    rows, width = queries.shape
    keys = key_rows.shape[0]
    pairs = width // PAIR
    big, _ = sizes(keys)
    qspec = pl.BlockSpec((rows, PAIR), lambda p, n: (0, p))
    kspec = pl.BlockSpec((keys, PAIR), lambda p, n: (0, p))
    return pl.pallas_call(
        backward_kernel,
        grid_spec=pltpu.PrefetchScalarGridSpec(
            num_scalar_prefetch=1,
            grid=(pairs,),
            in_specs=[qspec] * 4 + [kspec] * 2 + [pl.BlockSpec((2, rows, keys), lambda p, n: (p, 0, 0))],
            out_specs=[qspec, kspec, kspec],
            scratch_shapes=[
                pltpu.VMEM((2, rows, PAIR), f32),
                pltpu.VMEM((PAIR, big), f32),
                pltpu.VMEM((PAIR, big), f32),
            ],
        ),
        out_shape=[
            jax.ShapeDtypeStruct((rows, width), f32),
            jax.ShapeDtypeStruct((keys, width), bf16),
            jax.ShapeDtypeStruct((keys, width), bf16),
        ],
        compiler_params=pltpu.CompilerParams(vmem_limit_bytes=VMEM),
        cost_estimate=pl.CostEstimate(
            flops=24 * rows * keys * width, bytes_accessed=2 * rows * keys * width // HEAD, transcendentals=0
        ),
        name="attention_backward",
    )(length, queries, grads, context, linv, key_rows, value_rows, weights)


def layer_norm(hidden):
    center = hidden - jnp.mean(hidden, -1, keepdims=True)
    inverse = lax.rsqrt(jnp.mean(center * center, -1, keepdims=True) + epsilon)
    return (center * inverse, inverse)


def norm_back(gradient, normed, inverse):
    return (
        gradient
        - jnp.mean(gradient, -1, keepdims=True)
        - normed * jnp.mean(gradient * normed, -1, keepdims=True)
    ) * inverse


def middle_kernel(part, chunk, x_ref, ctx_ref, cot_ref, wo_ref, wi_ref, wu_ref, ag_ref, fg_ref, ob_ref, as_ref, ib_ref, ub_ref, fs_ref,
                  out_ref, pre_ref, cg_ref, sum_ref, isum_ref, slope_ref):
    rows, width = x_ref.shape
    hidden_width = wi_ref.shape[1]
    cuts = [slice(c, c + chunk) for c in range(0, hidden_width, chunk)]
    def colsum(t): return jnp.sum(t, 0, keepdims=True)
    totals = {}
    def add(name, t):
        totals[name] = totals[name] + colsum(t) if name in totals else colsum(t)
    def stages(r):
        span = slice(r, r + part)
        branch = nn(ctx_ref[span], wo_ref[...]) + ob_ref[...]
        normed_one, inverse_one = layer_norm(x_ref[span].astype(f32) + branch)
        mid = normed_one * ag_ref[...] + as_ref[...]
        low = mid.astype(bf16)
        yield
        total = None
        held = None
        def finish(cut, h):
            e = jnp.exp2(h * h * (-0.5 * math.log2(math.e)))
            phi = 0.5 + 0.5 * lax.erf(h * math.sqrt(0.5))
            slope_ref[span, cut] = phi + h * (e * (1.0 / math.sqrt(2.0 * math.pi)))
            return nn((h * phi).astype(bf16), wu_ref[cut])
        for cut in cuts:
            h = nn(low, wi_ref[:, cut]) + ib_ref[:, cut]
            if held is not None:
                t = finish(*held); total = t if total is None else total + t
            held = (cut, h)
        t = finish(*held); total = t if total is None else total + t
        yield
        normed_two, inverse_two = layer_norm(mid + total + ub_ref[...])
        out_ref[span] = (normed_two * fg_ref[...] + fs_ref[...]).astype(bf16)
        cot = cot_ref[span].astype(f32)
        pre_two = norm_back(cot * fg_ref[...], normed_two, inverse_two)
        add("cot", cot); add("two", pre_two)
        low = pre_two.astype(bf16)
        yield
        total = pre_two
        held = None
        def back(cut, d):
            g = d * slope_ref[span, cut]
            add(("inner", cut.start), g)
            return nt(g.astype(bf16), wi_ref[:, cut])
        for cut in cuts:
            d = nt(low, wu_ref[cut])
            if held is not None: total = total + back(*held)
            held = (cut, d)
        total = total + back(*held)
        yield
        add("mid", total)
        pre_one = norm_back(total * ag_ref[...], normed_one, inverse_one)
        add("one", pre_one)
        pre_ref[span] = pre_one
        cg = nt(pre_one.astype(bf16), wo_ref[...])
        add("ctx", cg)
        cg_ref[span] = cg.astype(bf16)
        yield
    flows = [stages(r) for r in range(0, rows, part)]
    n = 5
    for t in range(n + len(flows) - 1):
        for i, f in enumerate(flows):
            if 0 <= t - i < n: next(f)
    for j, name in enumerate(("ctx", "one", "mid", "two", "cot")):
        sum_ref[j:j+1] = totals[name]
    for cut in cuts: isum_ref[0:1, cut] = totals[("inner", cut.start)]

def middle(x, ctx, cot, wo, wi, wu, ag, fg, ob, ash, ib, ub, fs, part=256, chunk=768):
    rows, width = x.shape
    hw = wi.shape[1]
    part=min(part,rows)
    v = lambda t: t.reshape(1, -1)
    return pl.pallas_call(functools.partial(middle_kernel, part, chunk),
        out_shape=[jax.ShapeDtypeStruct((rows, width), bf16), jax.ShapeDtypeStruct((rows, width), f32), jax.ShapeDtypeStruct((rows, width), bf16),
                   jax.ShapeDtypeStruct((8, width), f32), jax.ShapeDtypeStruct((8, hw), f32)],
        scratch_shapes=[pltpu.VMEM((rows, hw), f32)],
        compiler_params=pltpu.CompilerParams(vmem_limit_bytes=VMEM), name="middle_rows",
        cost_estimate=pl.CostEstimate(flops=8*rows*width*hw+4*rows*width*width, bytes_accessed=4*width*hw, transcendentals=0),
        )(x, ctx, cot, wo, wi, wu, v(ag), v(fg), v(ob), v(ash), v(ib), v(ub), v(fs))


X_PAIRS = [(0, 1), (1, 0), (2, 3), (3, 2)]
Y_PAIRS = [(0, 2), (2, 0), (1, 3), (3, 1)]


def over_x(block):
    return lax.ppermute(block, "seq", X_PAIRS)


def over_y(block):
    return lax.ppermute(block, "seq", Y_PAIRS)


def gather_rows(block, after):
    rows, width = block.shape
    count = lax.axis_size("seq")
    if count != 4:
        return lax.all_gather(block, "seq", axis=0, tiled=True), after
    device = lax.axis_index("seq")
    block, after = lax.optimization_barrier((block, after))
    by_x, by_y = over_x(block), over_y(block)
    half = rows // 2
    far = jnp.concatenate([over_x(by_y[:half]), over_y(by_x[half:])], 0)
    whole = jnp.zeros((count * rows, width), block.dtype)
    for r, piece in enumerate((block, by_x, by_y, far)):
        whole = lax.dynamic_update_slice(whole, piece, ((device ^ r) * rows, 0))
    return whole, (by_x, by_y)


def scatter_rows(partial):
    count = lax.axis_size("seq")
    rows = partial.shape[0] // count
    if count != 4:
        return lax.psum_scatter(partial, "seq", scatter_dimension=0, tiled=True).astype(f32)
    device = lax.axis_index("seq")
    own, to_x, to_y, far = (
        lax.dynamic_slice(partial, ((device ^ r) * rows, 0), (rows, partial.shape[1])) for r in range(4)
    )
    half = rows // 2
    got_x, got_y = over_x(far[:half]), over_y(far[half:])
    to_x = jnp.concatenate([to_x[:half], (to_x[half:].astype(f32) + got_y.astype(f32)).astype(bf16)], 0)
    to_y = jnp.concatenate([(to_y[:half].astype(f32) + got_x.astype(f32)).astype(bf16), to_y[half:]], 0)
    return own.astype(f32) + over_x(to_x).astype(f32) + over_y(to_y).astype(f32)


def sum_all(value):
    sizes_of = [(axis, lax.axis_size(axis)) for axis in ("seq", "dp")]
    if any(size & (size - 1) for _, size in sizes_of):
        return lax.psum(value, ("seq", "dp"))
    for axis, size in sizes_of:
        step = 1
        while step < size:
            value = value + lax.ppermute(value, axis, [(i, i ^ step) for i in range(size)])
            step *= 2
    return value


def local(
    inputs, cotangent, lengths, triple_weight, output_weight, inner_weight, outer_weight,
    attn_gain, ffn_gain, query_bias, value_bias, output_bias, attn_shift, inner_bias, outer_bias, ffn_shift,
):
    seq_count, tok_count, width = inputs.shape
    to_log2 = math.log2(math.e) / math.sqrt(HEAD)
    query_weight, pair_weight = triple_weight[:, :width], triple_weight[:, width:]
    pair_bias = jnp.concatenate([jnp.zeros_like(value_bias), value_bias])
    after = jnp.zeros((), f32)
    gathered = []
    for s in range(seq_count):
        whole, after = gather_rows(inputs[s], after)
        gathered.append(whole)
    outs, grads_in, sums, inner_sums, query_sums = [], [], [], [], []
    turn = jnp.zeros((), f32)
    for s in range(seq_count):
        length, whole, rows, _ = lax.optimization_barrier((lengths[s : s + 1], gathered[s], inputs[s], turn))
        queries = ((nn(rows, query_weight) + query_bias) * to_log2).astype(bf16)
        both = (nn(whole, pair_weight) + pair_bias).astype(bf16)
        key_rows, value_rows = both[:, :width], both[:, width:]
        weights, context, linv = attention_forward(length, queries, key_rows, value_rows)
        out, pre_one, context_grad, total, inner_total = middle(
            rows, context, cotangent[s], output_weight, inner_weight, outer_weight, attn_gain, ffn_gain,
            output_bias, attn_shift, inner_bias, outer_bias, ffn_shift,
        )
        outs.append(out)
        sums.append(total[:5].reshape(-1))
        inner_sums.append(inner_total[0])
        dq, dk, dv = attention_backward(
            length, queries, context_grad, context, linv, key_rows, value_rows, weights
        )
        turn = dq
        partial = (nt(dk, triple_weight[:, width : 2 * width]) + nt(dv, triple_weight[:, 2 * width :])).astype(bf16)
        grads_in.append((pre_one + nt(dq.astype(bf16), query_weight) + scatter_rows(partial)).astype(bf16))
        query_sums.append(jnp.sum(dq, 0))
    early = sum_all(jnp.concatenate([sum(sums), sum(inner_sums)]))
    query_bias_grad = sum_all(sum(query_sums))
    value_bias_grad, output_bias_grad, attn_shift_grad, outer_bias_grad, ffn_shift_grad = (
        early[i * width : (i + 1) * width] for i in range(5)
    )
    return (
        jnp.stack(outs), jnp.stack(grads_in), query_bias_grad, value_bias_grad, output_bias_grad,
        attn_shift_grad, early[5 * width :], outer_bias_grad, ffn_shift_grad,
    )


def solution(mesh):
    split = P("dp", "seq", None)
    return jax.shard_map(
        local,
        mesh=mesh,
        in_specs=(split, split, P("dp")) + (P(),) * 13,
        out_specs=(split, split) + (P(),) * 7,
        check_vma=False,
    )
```

```python
import functools
import math

import jax
import jax.numpy as jnp
from jax import lax
from jax.experimental import pallas as pl
from jax.experimental.pallas import tpu as pltpu
from jax.sharding import PartitionSpec as P

HEAD = 64
PAIR = 128
epsilon = 1e-06
NEG = -1e30
SUM_LOW, SUM_HIGH = 2.0**-90, 2.0**100
bf16, f32 = jnp.bfloat16, jnp.float32
VMEM = 56 << 20


def nn(a, b):
    return lax.dot_general(a, b, (((1,), (0,)), ((), ())), preferred_element_type=f32)


def nt(a, b):
    return lax.dot_general(a, b, (((1,), (1,)), ((), ())), preferred_element_type=f32)


def split3(value):
    first = value.astype(bf16).astype(f32)
    second = (value - first).astype(bf16).astype(f32)
    return first, second, value - first - second


def sizes(keys):
    return max(keys // 2, 128), max(keys // 4, 128)


def over_keys(length, keys, step):
    big, small = sizes(keys)
    count = (length + small - 1) // small
    ratio = big // small
    full = count // ratio

    def turn(i, carried):
        step(pl.multiple_of(i * big, big), big)
        return carried

    lax.fori_loop(0, full, turn, 0)
    if ratio > 1:

        @pl.when(count > full * ratio)
        def _():
            step(pl.multiple_of(full * big, small), small)


def pipelined(units, first, second):
    held = None
    for unit in units:
        result = first(unit)
        if held is not None:
            second(*held)
        held = (unit, result)
    second(*held)


def in_head(index, h):
    return (index >= HEAD) == (h == 1)


def forward_kernel(length_ref, q_ref, k_ref, v_ref, p_ref, ctx_ref, linv_ref, acc_ref, top_ref):
    length = length_ref[0]
    rows, keys = q_ref.shape[0], k_ref.shape[0]
    part = min(rows, 256)
    lane = lax.broadcasted_iota(jnp.int32, (rows, PAIR), 1)

    def queries(h, top):
        other = HEAD * (1 - h)
        a, b, c = split3(-top)
        extra = jnp.where(lane == other + 3, 1.0, 0.0)
        for j, piece in enumerate((a, b, c)):
            extra = jnp.where(lane == other + j, piece, extra)
        return jnp.where(in_head(lane, h), q_ref[...].astype(f32), extra).astype(bf16)

    def key_side(h, start, size):
        other = HEAD * (1 - h)
        at = lax.broadcasted_iota(jnp.int32, (size, PAIR), 1)
        place = start + lax.broadcasted_iota(jnp.int32, (size, PAIR), 0)
        extra = jnp.where(at == other + 3, jnp.where(place < length, 0.0, NEG), 1.0).astype(bf16)
        return jnp.where(in_head(at, h), k_ref[pl.ds(start, size)], extra).T

    def sweep(sides):
        acc_ref[...] = jnp.zeros_like(acc_ref)

        def step(start, size):
            at = lax.broadcasted_iota(jnp.int32, (size, PAIR), 1)
            values = v_ref[pl.ds(start, size)]
            one = jnp.ones((), bf16)
            kt = [key_side(h, start, size) for h in range(2)]
            va = [jnp.where(in_head(at, h), values, one) for h in range(2)]

            def score(unit):
                h, c = unit
                return nn(sides[h][c : c + part], kt[h])

            def weigh(unit, s):
                h, c = unit
                p = jnp.exp2(s).astype(bf16)
                p_ref[h, c : c + part, pl.ds(start, size)] = p
                acc_ref[h, c : c + part] += nn(p, va[h])

            pipelined([(h, c) for h in range(2) for c in range(0, rows, part)], score, weigh)

        over_keys(length, keys, step)

    zero = jnp.zeros((rows, 1), f32)
    plain = [queries(h, zero) for h in range(2)]
    sweep(plain)

    def sums():
        return jnp.where(lane < HEAD, acc_ref[1], acc_ref[0])

    total = sums()
    fine = jnp.logical_and(jnp.min(total) > SUM_LOW, jnp.max(total) < SUM_HIGH)

    @pl.when(jnp.logical_not(fine))
    def _():
        top_ref[...] = jnp.full_like(top_ref, NEG)

        def step(start, size):
            for h in range(2):
                s = nn(plain[h], key_side(h, start, size))
                top_ref[h] = jnp.maximum(top_ref[h], jnp.max(s, 1, keepdims=True))

        over_keys(length, keys, step)
        sweep([queries(h, top_ref[h][:, :1]) for h in range(2)])

    inverse = pltpu.roll(1.0 / sums(), HEAD, 1)
    linv_ref[...] = inverse
    ctx_ref[...] = (jnp.where(lane < HEAD, acc_ref[0], acc_ref[1]) * inverse).astype(bf16)


def attention_forward(length, queries, key_rows, value_rows):
    rows, width = queries.shape
    keys = key_rows.shape[0]
    pairs = width // PAIR
    qspec = pl.BlockSpec((rows, PAIR), lambda p, n: (0, p))
    kspec = pl.BlockSpec((keys, PAIR), lambda p, n: (0, p))
    return pl.pallas_call(
        forward_kernel,
        grid_spec=pltpu.PrefetchScalarGridSpec(
            num_scalar_prefetch=1,
            grid=(pairs,),
            in_specs=[qspec, kspec, kspec],
            out_specs=[pl.BlockSpec((2, rows, keys), lambda p, n: (p, 0, 0)), qspec, qspec],
            scratch_shapes=[pltpu.VMEM((2, rows, PAIR), f32), pltpu.VMEM((2, rows, PAIR), f32)],
        ),
        out_shape=[
            jax.ShapeDtypeStruct((2 * pairs, rows, keys), bf16),
            jax.ShapeDtypeStruct((rows, width), bf16),
            jax.ShapeDtypeStruct((rows, width), f32),
        ],
        compiler_params=pltpu.CompilerParams(vmem_limit_bytes=VMEM),
        cost_estimate=pl.CostEstimate(
            flops=16 * rows * keys * width, bytes_accessed=2 * rows * keys * width // HEAD, transcendentals=0
        ),
        name="attention_forward",
    )(length, queries, key_rows, value_rows)


def backward_kernel(
    length_ref, q_ref, g_ref, ctx_ref, linv_ref, k_ref, v_ref, p_ref,
    dq_ref, dk_ref, dv_ref, acc_ref, dkt_ref, dvt_ref,
):
    length = length_ref[0]
    rows, keys = q_ref.shape[0], k_ref.shape[0]
    lane = lax.broadcasted_iota(jnp.int32, (rows, PAIR), 1)
    grad = g_ref[...].astype(f32)
    inverse = linv_ref[...]
    product = grad * ctx_ref[...].astype(f32) * inverse
    scaled = grad * inverse
    sides = []
    for h in range(2):
        other = HEAD * (1 - h)
        delta = jnp.sum(jnp.where(in_head(lane, h), product, 0.0), 1, keepdims=True)
        extra = jnp.zeros((rows, PAIR), f32)
        for j, piece in enumerate(split3(-delta)):
            extra = jnp.where(lane == other + j, piece, extra)
        sides.append(jnp.where(in_head(lane, h), scaled, extra).astype(bf16))
    gt = scaled.astype(bf16).T
    qt = q_ref[...].T
    acc_ref[...] = jnp.zeros_like(acc_ref)
    big, small = sizes(keys)
    count = (length + small - 1) // small

    def step(start, size):
        at = lax.broadcasted_iota(jnp.int32, (size, PAIR), 1)
        span = pl.ds(start, size)
        key_rows, value_rows = k_ref[span], v_ref[span]
        one = jnp.ones((), bf16)
        vt = [jnp.where(in_head(at, h), value_rows, one).T for h in range(2)]

        def first(h):
            return nn(sides[h], vt[h])

        def second(h, dp):
            p = p_ref[h, :, span]
            ds = (p.astype(f32) * dp).astype(bf16)
            acc_ref[h] += nn(ds, key_rows)
            mine = slice(HEAD * h, HEAD * h + HEAD)
            dvt_ref[mine, :size] = nn(gt, p)[mine]
            dkt_ref[mine, :size] = nn(qt, ds)[mine]

        pipelined(range(2), first, second)
        dk_ref[span] = (dkt_ref[:, :size] * math.log(2.0)).astype(bf16).T
        dv_ref[span] = dvt_ref[:, :size].astype(bf16).T

    over_keys(length, keys, step)

    def blank(i, carried):
        span = pl.ds(pl.multiple_of(i * small, small), small)
        dk_ref[span] = jnp.zeros((small, PAIR), bf16)
        dv_ref[span] = jnp.zeros((small, PAIR), bf16)
        return carried

    lax.fori_loop(count, keys // small, blank, 0)
    dq_ref[...] = jnp.where(lane < HEAD, acc_ref[0], acc_ref[1]) * (1.0 / math.sqrt(HEAD))


def attention_backward(length, queries, grads, context, linv, key_rows, value_rows, weights):
    rows, width = queries.shape
    keys = key_rows.shape[0]
    pairs = width // PAIR
    big, _ = sizes(keys)
    qspec = pl.BlockSpec((rows, PAIR), lambda p, n: (0, p))
    kspec = pl.BlockSpec((keys, PAIR), lambda p, n: (0, p))
    return pl.pallas_call(
        backward_kernel,
        grid_spec=pltpu.PrefetchScalarGridSpec(
            num_scalar_prefetch=1,
            grid=(pairs,),
            in_specs=[qspec] * 4 + [kspec] * 2 + [pl.BlockSpec((2, rows, keys), lambda p, n: (p, 0, 0))],
            out_specs=[qspec, kspec, kspec],
            scratch_shapes=[
                pltpu.VMEM((2, rows, PAIR), f32),
                pltpu.VMEM((PAIR, big), f32),
                pltpu.VMEM((PAIR, big), f32),
            ],
        ),
        out_shape=[
            jax.ShapeDtypeStruct((rows, width), f32),
            jax.ShapeDtypeStruct((keys, width), bf16),
            jax.ShapeDtypeStruct((keys, width), bf16),
        ],
        compiler_params=pltpu.CompilerParams(vmem_limit_bytes=VMEM),
        cost_estimate=pl.CostEstimate(
            flops=24 * rows * keys * width, bytes_accessed=2 * rows * keys * width // HEAD, transcendentals=0
        ),
        name="attention_backward",
    )(length, queries, grads, context, linv, key_rows, value_rows, weights)


def layer_norm(hidden):
    center = hidden - jnp.mean(hidden, -1, keepdims=True)
    inverse = lax.rsqrt(jnp.mean(center * center, -1, keepdims=True) + epsilon)
    return (center * inverse, inverse)


def norm_back(gradient, normed, inverse):
    return (
        gradient
        - jnp.mean(gradient, -1, keepdims=True)
        - normed * jnp.mean(gradient * normed, -1, keepdims=True)
    ) * inverse


def middle_kernel(part, chunk, x_ref, ctx_ref, cot_ref, wo_ref, wi_ref, wu_ref, ag_ref, fg_ref, ob_ref, as_ref, ib_ref, ub_ref, fs_ref,
                  out_ref, pre_ref, cg_ref, sum_ref, isum_ref, slope_ref):
    rows, width = x_ref.shape
    hidden_width = wi_ref.shape[1]
    cuts = [slice(c, c + chunk) for c in range(0, hidden_width, chunk)]
    def colsum(t): return jnp.sum(t, 0, keepdims=True)
    totals = {}
    def add(name, t):
        totals[name] = totals[name] + colsum(t) if name in totals else colsum(t)
    def stages(r):
        span = slice(r, r + part)
        branch = nn(ctx_ref[span], wo_ref[...]) + ob_ref[...]
        normed_one, inverse_one = layer_norm(x_ref[span].astype(f32) + branch)
        mid = normed_one * ag_ref[...] + as_ref[...]
        low = mid.astype(bf16)
        yield
        total = None
        held = None
        def finish(cut, h):
            e = jnp.exp2(h * h * (-0.5 * math.log2(math.e)))
            phi = 0.5 + 0.5 * lax.erf(h * math.sqrt(0.5))
            slope_ref[span, cut] = phi + h * (e * (1.0 / math.sqrt(2.0 * math.pi)))
            return nn((h * phi).astype(bf16), wu_ref[cut])
        for cut in cuts:
            h = nn(low, wi_ref[:, cut]) + ib_ref[:, cut]
            if held is not None:
                t = finish(*held); total = t if total is None else total + t
            held = (cut, h)
        t = finish(*held); total = t if total is None else total + t
        yield
        normed_two, inverse_two = layer_norm(mid + total + ub_ref[...])
        out_ref[span] = (normed_two * fg_ref[...] + fs_ref[...]).astype(bf16)
        cot = cot_ref[span].astype(f32)
        pre_two = norm_back(cot * fg_ref[...], normed_two, inverse_two)
        add("cot", cot); add("two", pre_two)
        low = pre_two.astype(bf16)
        yield
        total = pre_two
        held = None
        def back(cut, d):
            g = d * slope_ref[span, cut]
            add(("inner", cut.start), g)
            return nt(g.astype(bf16), wi_ref[:, cut])
        for cut in cuts:
            d = nt(low, wu_ref[cut])
            if held is not None: total = total + back(*held)
            held = (cut, d)
        total = total + back(*held)
        yield
        add("mid", total)
        pre_one = norm_back(total * ag_ref[...], normed_one, inverse_one)
        add("one", pre_one)
        pre_ref[span] = pre_one
        cg = nt(pre_one.astype(bf16), wo_ref[...])
        add("ctx", cg)
        cg_ref[span] = cg.astype(bf16)
        yield
    flows = [stages(r) for r in range(0, rows, part)]
    n = 5
    for t in range(n + len(flows) - 1):
        for i, f in enumerate(flows):
            if 0 <= t - i < n: next(f)
    for j, name in enumerate(("ctx", "one", "mid", "two", "cot")):
        sum_ref[j:j+1] = totals[name]
    for cut in cuts: isum_ref[0:1, cut] = totals[("inner", cut.start)]

def middle(seq, x, ctx, cot, earlier, wo, wi, wu, ag, fg, ob, ash, ib, ub, fs, part=256, chunk=768):
    _, rows, width = x.shape
    hw = wi.shape[1]
    part = min(part, rows)
    mine = pl.BlockSpec((None, rows, width), lambda i: (seq, 0, 0))

    def whole(t):
        return pl.BlockSpec(t.shape, lambda i: (0,) * t.ndim)

    vectors = [v.reshape(1, -1) for v in (ag, fg, ob, ash, ib, ub, fs)]
    operands = [x, ctx, cot, wo, wi, wu, *vectors]
    specs = [mine, whole(ctx), mine] + [whole(t) for t in operands[3:]]
    kernel = functools.partial(middle_kernel, part, chunk)
    alias = {}
    if earlier is not None:
        operands.append(earlier)
        specs.append(pl.BlockSpec(memory_space=pl.ANY))
        alias = {len(operands) - 1: 0}
        plain = kernel

        def kernel(*refs):
            plain(*refs[: len(operands) - 1], *refs[len(operands) :])

    flat = jax.ShapeDtypeStruct((rows, width), f32)
    outs = [jax.ShapeDtypeStruct(x.shape, bf16), flat, jax.ShapeDtypeStruct((rows, width), bf16)]
    outs += [jax.ShapeDtypeStruct((8, width), f32), jax.ShapeDtypeStruct((8, hw), f32)]
    return pl.pallas_call(
        kernel,
        grid=(1,),
        in_specs=specs,
        out_specs=[mine] + [whole(t) for t in outs[1:]],
        out_shape=outs,
        scratch_shapes=[pltpu.VMEM((rows, hw), f32)],
        input_output_aliases=alias,
        compiler_params=pltpu.CompilerParams(vmem_limit_bytes=VMEM),
        name="middle_rows",
        cost_estimate=pl.CostEstimate(
            flops=8 * rows * width * (2 * hw + width), bytes_accessed=4 * width * hw, transcendentals=0
        ),
    )(*operands)


def project_kernel(meta_ref, x0, x1, x2, x3, w_ref, qb_ref, vb_ref, q_ref, k_ref, v_ref):
    r = pl.program_id(0)
    rows, width = x0.shape
    to_log2 = math.log2(math.e) / math.sqrt(HEAD)
    wanted = meta_ref[1 + r] * rows < meta_ref[0]
    for j, x in enumerate((x0, x1, x2, x3)):

        @pl.when(jnp.logical_and(r == j, wanted))
        def _(x=x):
            k_ref[...] = nn(x[...], w_ref[:, width : 2 * width]).astype(bf16)
            v_ref[...] = (nn(x[...], w_ref[:, 2 * width :]) + vb_ref[...]).astype(bf16)

    @pl.when(jnp.logical_not(wanted))
    def _():
        k_ref[...] = jnp.zeros_like(k_ref)
        v_ref[...] = jnp.zeros_like(v_ref)

    @pl.when(r == 0)
    def _():
        q_ref[...] = ((nn(x0[...], w_ref[:, :width]) + qb_ref[...]) * to_log2).astype(bf16)


def project(meta, blocks, weight, query_bias, value_bias):
    rows, width = blocks[0].shape

    def whole(t):
        return pl.BlockSpec(t.shape, lambda r, m: (0,) * t.ndim)

    operands = [*blocks, weight, query_bias.reshape(1, -1), value_bias.reshape(1, -1)]
    owned = pl.BlockSpec((rows, width), lambda r, m: (m[1 + r], 0))
    all_keys = jax.ShapeDtypeStruct((4 * rows, width), bf16)
    return pl.pallas_call(
        project_kernel,
        grid_spec=pltpu.PrefetchScalarGridSpec(
            num_scalar_prefetch=1,
            grid=(4,),
            in_specs=[whole(t) for t in operands],
            out_specs=[pl.BlockSpec((rows, width), lambda r, m: (0, 0)), owned, owned],
        ),
        out_shape=[jax.ShapeDtypeStruct((rows, width), bf16), all_keys, all_keys],
        compiler_params=pltpu.CompilerParams(vmem_limit_bytes=VMEM),
        name="project",
        cost_estimate=pl.CostEstimate(
            flops=18 * rows * width * width, bytes_accessed=12 * rows * width, transcendentals=0
        ),
    )(meta, *operands)


def input_kernel(meta_ref, pre_ref, dq_ref, dk_ref, dv_ref, w_ref, own_ref, x_ref, y_ref, far_ref, sum_ref):
    step = pl.program_id(0)
    r = 3 - step
    rows, width = pre_ref.shape
    wanted = meta_ref[1 + r] * rows < meta_ref[0]

    def terms():
        return nt(dk_ref[...], w_ref[:, width : 2 * width]) + nt(dv_ref[...], w_ref[:, 2 * width :])

    for j, out in ((3, far_ref), (2, y_ref), (1, x_ref)):

        @pl.when(jnp.logical_and(r == j, wanted))
        def _(out=out):
            out[...] = terms().astype(bf16)

        @pl.when(jnp.logical_and(r == j, jnp.logical_not(wanted)))
        def _(out=out):
            out[...] = jnp.zeros_like(out)

    @pl.when(r == 0)
    def _():
        dq = dq_ref[...]
        own_ref[...] = pre_ref[...] + nt(dq.astype(bf16), w_ref[:, :width])
        sum_ref[0:1] = jnp.sum(dq, 0, keepdims=True)

    @pl.when(jnp.logical_and(r == 0, wanted))
    def _():
        own_ref[...] += terms()


def input_parts(meta, pre_one, dq, dk, dv, weight):
    rows, width = pre_one.shape

    def whole(shape):
        return pl.BlockSpec(shape, lambda i, m: (0, 0))

    owned = pl.BlockSpec((rows, width), lambda i, m: (m[4 - i], 0))
    part = jax.ShapeDtypeStruct((rows, width), bf16)
    outs = [jax.ShapeDtypeStruct((rows, width), f32), part, part, part, jax.ShapeDtypeStruct((8, width), f32)]
    return pl.pallas_call(
        input_kernel,
        grid_spec=pltpu.PrefetchScalarGridSpec(
            num_scalar_prefetch=1,
            grid=(4,),
            in_specs=[whole(pre_one.shape), whole(dq.shape), owned, owned, whole(weight.shape)],
            out_specs=[whole(t.shape) for t in outs],
        ),
        out_shape=outs,
        compiler_params=pltpu.CompilerParams(vmem_limit_bytes=VMEM),
        name="input_parts",
        cost_estimate=pl.CostEstimate(
            flops=18 * rows * width * width, bytes_accessed=12 * rows * width, transcendentals=0
        ),
    )(meta, pre_one, dq, dk, dv, weight)


X_PAIRS = [(0, 1), (1, 0), (2, 3), (3, 2)]
Y_PAIRS = [(0, 2), (2, 0), (1, 3), (3, 1)]


def over_x(block):
    return lax.ppermute(block, "seq", X_PAIRS)


def over_y(block):
    return lax.ppermute(block, "seq", Y_PAIRS)


def sum_all(value):
    sizes_of = [(axis, lax.axis_size(axis)) for axis in ("seq", "dp")]
    if any(size & (size - 1) for _, size in sizes_of):
        return lax.psum(value, ("seq", "dp"))
    for axis, size in sizes_of:
        step = 1
        while step < size:
            value = value + lax.ppermute(value, axis, [(i, i ^ step) for i in range(size)])
            step *= 2
    return value


def fence(values, *others):
    return lax.optimization_barrier((values, *others))[0]


def local(
    inputs, cotangent, lengths, triple_weight, output_weight, inner_weight, outer_weight,
    attn_gain, ffn_gain, query_bias, value_bias, output_bias, attn_shift, inner_bias, outer_bias, ffn_shift,
):
    seq_count, tok_count, width = inputs.shape
    half = tok_count // 2
    square = lax.axis_size("seq") == 4
    device = lax.axis_index("seq")
    owners = device ^ jnp.arange(4, dtype=jnp.int32)
    metas = [jnp.concatenate([lengths[s : s + 1], owners]) for s in range(seq_count)]
    by_x, by_y, far = {}, {}, {}

    def exchange(s, *after):
        block = fence(inputs[s], *after)
        by_x[s], by_y[s] = over_x(block), over_y(block)

    def relay(s):
        far[s] = jnp.concatenate([over_x(by_y[s][:half]), over_y(by_x[s][half:])], 0)

    def start(s, *after):
        rows = inputs[s]
        if square:
            blocks = fence((rows, by_x[s], by_y[s], far[s]), *after)
            return project(metas[s], blocks, triple_weight, query_bias, value_bias)
        rows = fence(rows, *after)
        to_log2 = math.log2(math.e) / math.sqrt(HEAD)
        queries = ((nn(rows, triple_weight[:, :width]) + query_bias) * to_log2).astype(bf16)
        whole = lax.all_gather(rows, "seq", axis=0, tiled=True)
        key_rows = nn(whole, triple_weight[:, width : 2 * width]).astype(bf16)
        value_rows = (nn(whole, triple_weight[:, 2 * width :]) + value_bias).astype(bf16)
        return queries, key_rows, value_rows

    grads_in = jnp.zeros(inputs.shape, bf16)
    layer_out = None
    sums, inner_sums, query_sums = [], [], []
    pending = None
    if square:
        exchange(0)
        relay(0)
        exchange(1, far[0])
    turn = ()
    for s in range(seq_count):
        last = s == seq_count - 1
        queries, key_rows, value_rows = start(s, *turn)
        length = lengths[s : s + 1]
        if square and s == 1 and 2 in far:
            queries = fence(queries, far[2])
        weights, context, linv = attention_forward(length, queries, key_rows, value_rows)
        if square and s == 0:
            context = fence(context, by_x[1], by_y[1])
            relay(1)
        if square and pending is not None:
            own, to_x, to_y, got_x, got_y = pending
            to_x = jnp.concatenate([to_x[:half], (to_x[half:].astype(f32) + got_y.astype(f32)).astype(bf16)], 0)
            to_y = jnp.concatenate([(to_y[:half].astype(f32) + got_x.astype(f32)).astype(bf16), to_y[half:]], 0)
            context, to_x, to_y = lax.optimization_barrier((context, to_x, to_y))
            ends = (over_x(to_x), over_y(to_y))
        layer_out, pre_one, context_grad, total, inner_total = middle(
            s, inputs, context, cotangent, layer_out, output_weight, inner_weight, outer_weight, attn_gain,
            ffn_gain, output_bias, attn_shift, inner_bias, outer_bias, ffn_shift,
        )
        sums.append(total[:5].reshape(-1))
        inner_sums.append(inner_total[0])
        if square and s == 0:
            context_grad = fence(context_grad, far[1])
            if seq_count > 2:
                exchange(2, far[1])
        if square and pending is not None:
            context_grad, *ends = lax.optimization_barrier((context_grad, *ends))
            result = (own + ends[0].astype(f32) + ends[1].astype(f32)).astype(bf16)
            grads_in = lax.dynamic_update_slice(grads_in, result[None], (s - 1, 0, 0))
        dq, dk, dv = attention_backward(
            length, queries, context_grad, context, linv, key_rows, value_rows, weights
        )
        if square and s == 0 and seq_count > 2:
            dq = fence(dq, by_x[2], by_y[2])
            relay(2)
        if square:
            own, to_x, to_y, across, query_total = input_parts(metas[s], pre_one, dq, dk, dv, triple_weight)
            query_sums.append(query_total[0])
            pending = own, to_x, to_y, over_x(across[:half]), over_y(across[half:])
            turn = (own,)
        else:
            partial = nt(dk, triple_weight[:, width : 2 * width]) + nt(dv, triple_weight[:, 2 * width :])
            summed = lax.psum_scatter(partial.astype(bf16), "seq", scatter_dimension=0, tiled=True).astype(f32)
            result = (pre_one + nt(dq.astype(bf16), triple_weight[:, :width]) + summed).astype(bf16)
            grads_in = lax.dynamic_update_slice(grads_in, result[None], (s, 0, 0))
            query_sums.append(jnp.sum(dq, 0))
            turn = (dq,)
    bias_sums = sum_all(jnp.concatenate([sum(query_sums), sum(sums), sum(inner_sums)]))
    if square:
        own, to_x, to_y, got_x, got_y = pending
        to_x = jnp.concatenate([to_x[:half], (to_x[half:].astype(f32) + got_y.astype(f32)).astype(bf16)], 0)
        to_y = jnp.concatenate([(to_y[:half].astype(f32) + got_x.astype(f32)).astype(bf16), to_y[half:]], 0)
        result = (own + over_x(to_x).astype(f32) + over_y(to_y).astype(f32)).astype(bf16)
        grads_in = lax.dynamic_update_slice(grads_in, result[None], (seq_count - 1, 0, 0))
    query_bias_grad, value_bias_grad, output_bias_grad, attn_shift_grad, outer_bias_grad, ffn_shift_grad = (
        bias_sums[i * width : (i + 1) * width] for i in range(6)
    )
    return (
        layer_out, grads_in, query_bias_grad, value_bias_grad, output_bias_grad,
        attn_shift_grad, bias_sums[6 * width :], outer_bias_grad, ffn_shift_grad,
    )


def solution(mesh):
    split = P("dp", "seq", None)
    return jax.shard_map(
        local,
        mesh=mesh,
        in_specs=(split, split, P("dp")) + (P(),) * 13,
        out_specs=(split, split) + (P(),) * 7,
        check_vma=False,
    )
```

```python
import functools
import math

import jax
import jax.numpy as jnp
from jax import lax
from jax.experimental import pallas as pl
from jax.experimental.pallas import tpu as pltpu
from jax.sharding import PartitionSpec as P

HEAD = 64
PAIR = 128
epsilon = 1e-06
NEG = -1e30
SUM_LOW, SUM_HIGH = 2.0**-90, 2.0**100
bf16, f32 = jnp.bfloat16, jnp.float32
FRONT_VMEM, BACK_VMEM = 60 << 20, 56 << 20


def nn(a, b):
    return lax.dot_general(a, b, (((1,), (0,)), ((), ())), preferred_element_type=f32)


def nt(a, b):
    return lax.dot_general(a, b, (((1,), (1,)), ((), ())), preferred_element_type=f32)


def split3(value):
    first = value.astype(bf16).astype(f32)
    second = (value - first).astype(bf16).astype(f32)
    return first, second, value - first - second


def sizes(keys):
    return max(keys // 2, 128), max(keys // 4, 128)


def over_keys(length, keys, step):
    big, small = sizes(keys)
    count = (length + small - 1) // small
    ratio = big // small
    full = count // ratio

    def turn(i, carried):
        step(pl.multiple_of(i * big, big), big)
        return carried

    lax.fori_loop(0, full, turn, 0)
    if ratio > 1:

        @pl.when(count > full * ratio)
        def _():
            step(pl.multiple_of(full * big, small), small)


def pipelined(units, first, second):
    held = None
    for unit in units:
        result = first(unit)
        if held is not None:
            second(*held)
        held = (unit, result)
    second(*held)


def in_head(index, h):
    return (index >= HEAD) == (h == 1)


def attend(pair, length, q_ref, k_ref, v_ref, p_ref, ctx_ref, linv_ref, acc_ref, top_ref):
    rows, keys = q_ref.shape[0], k_ref.shape[0]
    part = min(rows, 256)
    lanes = pl.ds(pl.multiple_of(pair * PAIR, PAIR), PAIR)
    lane = lax.broadcasted_iota(jnp.int32, (rows, PAIR), 1)

    def queries(h, top):
        other = HEAD * (1 - h)
        a, b, c = split3(-top)
        extra = jnp.where(lane == other + 3, 1.0, 0.0)
        for j, piece in enumerate((a, b, c)):
            extra = jnp.where(lane == other + j, piece, extra)
        return jnp.where(in_head(lane, h), q_ref[:, lanes].astype(f32), extra).astype(bf16)

    def key_side(h, start, size):
        other = HEAD * (1 - h)
        at = lax.broadcasted_iota(jnp.int32, (size, PAIR), 1)
        place = start + lax.broadcasted_iota(jnp.int32, (size, PAIR), 0)
        extra = jnp.where(at == other + 3, jnp.where(place < length, 0.0, NEG), 1.0).astype(bf16)
        return jnp.where(in_head(at, h), k_ref[pl.ds(start, size), lanes], extra).T

    def sweep(sides):
        acc_ref[...] = jnp.zeros_like(acc_ref)

        def step(start, size):
            at = lax.broadcasted_iota(jnp.int32, (size, PAIR), 1)
            values = v_ref[pl.ds(start, size), lanes]
            one = jnp.ones((), bf16)
            kt = [key_side(h, start, size) for h in range(2)]
            va = [jnp.where(in_head(at, h), values, one) for h in range(2)]

            def score(unit):
                h, c = unit
                return nn(sides[h][c : c + part], kt[h])

            def weigh(unit, s):
                h, c = unit
                p = jnp.exp2(s).astype(bf16)
                p_ref[h, c : c + part, pl.ds(start, size)] = p
                acc_ref[h, c : c + part] += nn(p, va[h])

            pipelined([(h, c) for h in range(2) for c in range(0, rows, part)], score, weigh)

        over_keys(length, keys, step)

    zero = jnp.zeros((rows, 1), f32)
    plain = [queries(h, zero) for h in range(2)]
    sweep(plain)

    def sums():
        return jnp.where(lane < HEAD, acc_ref[1], acc_ref[0])

    total = sums()
    fine = jnp.logical_and(jnp.min(total) > SUM_LOW, jnp.max(total) < SUM_HIGH)

    @pl.when(jnp.logical_not(fine))
    def _():
        top_ref[...] = jnp.full_like(top_ref, NEG)

        def step(start, size):
            for h in range(2):
                s = nn(plain[h], key_side(h, start, size))
                top_ref[h] = jnp.maximum(top_ref[h], jnp.max(s, 1, keepdims=True))

        over_keys(length, keys, step)
        sweep([queries(h, top_ref[h][:, :1]) for h in range(2)])

    inverse = pltpu.roll(1.0 / sums(), HEAD, 1)
    across = inverse.T
    linv_ref[pair, 0:1] = across[0:1]
    linv_ref[pair, 1:2] = across[HEAD : HEAD + 1]
    ctx_ref[:, lanes] = (jnp.where(lane < HEAD, acc_ref[0], acc_ref[1]) * inverse).astype(bf16)


def attend_back(
    pair, length, q_ref, g_ref, ctx_ref, linv_ref, k_ref, v_ref, p_ref,
    dq_ref, dk_ref, dv_ref, acc_ref, dkt_ref, dvt_ref,
):
    rows, keys = q_ref.shape[0], k_ref.shape[0]
    lanes = pl.ds(pl.multiple_of(pair * PAIR, PAIR), PAIR)
    lane = lax.broadcasted_iota(jnp.int32, (rows, PAIR), 1)
    grad = g_ref[...].astype(f32)
    inverse = jnp.concatenate(
        [jnp.broadcast_to(linv_ref[pair, h : h + 1], (HEAD, rows)) for h in range(2)], 0
    ).T
    product = grad * ctx_ref[...].astype(f32) * inverse
    scaled = grad * inverse
    sides = []
    for h in range(2):
        other = HEAD * (1 - h)
        delta = jnp.sum(jnp.where(in_head(lane, h), product, 0.0), 1, keepdims=True)
        extra = jnp.zeros((rows, PAIR), f32)
        for j, piece in enumerate(split3(-delta)):
            extra = jnp.where(lane == other + j, piece, extra)
        sides.append(jnp.where(in_head(lane, h), scaled, extra).astype(bf16))
    gt = scaled.astype(bf16).T
    qt = q_ref[...].T
    acc_ref[...] = jnp.zeros_like(acc_ref)
    big, small = sizes(keys)
    count = (length + small - 1) // small

    def step(start, size):
        at = lax.broadcasted_iota(jnp.int32, (size, PAIR), 1)
        span = pl.ds(start, size)
        key_rows, value_rows = k_ref[span], v_ref[span]
        one = jnp.ones((), bf16)
        vt = [jnp.where(in_head(at, h), value_rows, one).T for h in range(2)]

        def first(h):
            return nn(sides[h], vt[h])

        def second(h, dp):
            p = p_ref[h, :, span]
            ds = (p.astype(f32) * dp).astype(bf16)
            acc_ref[h] += nn(ds, key_rows)
            mine = slice(HEAD * h, HEAD * h + HEAD)
            dvt_ref[mine, :size] = nn(gt, p)[mine]
            dkt_ref[mine, :size] = nn(qt, ds)[mine]

        pipelined(range(2), first, second)
        dk_ref[span, lanes] = (dkt_ref[:, :size] * math.log(2.0)).astype(bf16).T
        dv_ref[span, lanes] = dvt_ref[:, :size].astype(bf16).T

    over_keys(length, keys, step)

    def blank(i, carried):
        span = pl.ds(pl.multiple_of(i * small, small), small)
        dk_ref[span, lanes] = jnp.zeros((small, PAIR), bf16)
        dv_ref[span, lanes] = jnp.zeros((small, PAIR), bf16)
        return carried

    lax.fori_loop(count, keys // small, blank, 0)
    dq_ref[:, lanes] = jnp.where(lane < HEAD, acc_ref[0], acc_ref[1]) * (1.0 / math.sqrt(HEAD))


def layer_norm(hidden):
    center = hidden - jnp.mean(hidden, -1, keepdims=True)
    inverse = lax.rsqrt(jnp.mean(center * center, -1, keepdims=True) + epsilon)
    return (center * inverse, inverse)


def norm_back(gradient, normed, inverse):
    return (
        gradient
        - jnp.mean(gradient, -1, keepdims=True)
        - normed * jnp.mean(gradient * normed, -1, keepdims=True)
    ) * inverse


def middle_kernel(part, chunk, x_ref, ctx_ref, cot_ref, wo_ref, wi_ref, wu_ref, ag_ref, fg_ref, ob_ref, as_ref, ib_ref, ub_ref, fs_ref,
                  out_ref, pre_ref, cg_ref, sum_ref, isum_ref, slope_ref):
    rows, width = x_ref.shape
    hidden_width = wi_ref.shape[1]
    cuts = [slice(c, c + chunk) for c in range(0, hidden_width, chunk)]
    def colsum(t): return jnp.sum(t, 0, keepdims=True)
    totals = {}
    def add(name, t):
        totals[name] = totals[name] + colsum(t) if name in totals else colsum(t)
    def stages(r):
        span = slice(r, r + part)
        branch = nn(ctx_ref[span], wo_ref[...]) + ob_ref[...]
        normed_one, inverse_one = layer_norm(x_ref[span].astype(f32) + branch)
        mid = normed_one * ag_ref[...] + as_ref[...]
        low = mid.astype(bf16)
        yield
        total = None
        held = None
        def finish(cut, h):
            e = jnp.exp2(h * h * (-0.5 * math.log2(math.e)))
            phi = 0.5 + 0.5 * lax.erf(h * math.sqrt(0.5))
            slope_ref[span, cut] = phi + h * (e * (1.0 / math.sqrt(2.0 * math.pi)))
            return nn((h * phi).astype(bf16), wu_ref[cut])
        for cut in cuts:
            h = nn(low, wi_ref[:, cut]) + ib_ref[:, cut]
            if held is not None:
                t = finish(*held); total = t if total is None else total + t
            held = (cut, h)
        t = finish(*held); total = t if total is None else total + t
        yield
        normed_two, inverse_two = layer_norm(mid + total + ub_ref[...])
        out_ref[span] = (normed_two * fg_ref[...] + fs_ref[...]).astype(bf16)
        cot = cot_ref[span].astype(f32)
        pre_two = norm_back(cot * fg_ref[...], normed_two, inverse_two)
        add("cot", cot); add("two", pre_two)
        low = pre_two.astype(bf16)
        yield
        total = pre_two
        held = None
        def back(cut, d):
            g = d * slope_ref[span, cut]
            add(("inner", cut.start), g)
            return nt(g.astype(bf16), wi_ref[:, cut])
        for cut in cuts:
            d = nt(low, wu_ref[cut])
            if held is not None: total = total + back(*held)
            held = (cut, d)
        total = total + back(*held)
        yield
        add("mid", total)
        pre_one = norm_back(total * ag_ref[...], normed_one, inverse_one)
        add("one", pre_one)
        pre_ref[span] = pre_one
        cg = nt(pre_one.astype(bf16), wo_ref[...])
        add("ctx", cg)
        cg_ref[span] = cg.astype(bf16)
        yield
    flows = [stages(r) for r in range(0, rows, part)]
    n = 5
    for t in range(n + len(flows) - 1):
        for i, f in enumerate(flows):
            if 0 <= t - i < n: next(f)
    for j, name in enumerate(("ctx", "one", "mid", "two", "cot")):
        sum_ref[j:j+1] = totals[name]
    for cut in cuts: isum_ref[0:1, cut] = totals[("inner", cut.start)]

BLOCKS = 4


def front_kernel(part, chunk, seq, whole_block, count, meta_ref, x_ref, *refs):
    pieces, refs = refs[:count], refs[count:]
    (
        cot_hbm, w_hbm, wo_hbm, wi_hbm, wu_hbm,
        qb_ref, vb_ref, ag_ref, fg_ref, ob_ref, as_ref, ib_ref, ub_ref, fs_ref,
    ) = refs[:14]
    (
        out_ref, q_ref, k_hbm, v_hbm, p_hbm, ctx_ref, linv_ref, pre_ref, cg_ref, sum_ref, isum_ref,
        xs, w, wo, wi, wu, cot, k_all, v_all, p_two, acc_ref, top_ref, slope_ref, sems, p_sems,
    ) = refs[-25:]
    step = pl.program_id(0)
    pairs = p_hbm.shape[0] // 2
    block, width = xs.shape[1:]
    length = meta_ref[0]
    side = [slice(j * width, (j + 1) * width) for j in range(3)]
    load_x = []
    for j in range(BLOCKS):
        if whole_block:
            parts = [(pieces[0].at[pl.ds(j * block, block)], xs.at[j])]
        elif j == 0:
            parts = [(pieces[0].at[seq], xs.at[0])]
        else:
            half = block // 2
            parts = [(pieces[2 * j - 1 + i], xs.at[j, pl.ds(i * half, half)]) for i in range(2)]
        load_x.append([pltpu.make_async_copy(src, dst, sems.at[13 + 2 * j + i]) for i, (src, dst) in enumerate(parts)])
    load_w = [pltpu.make_async_copy(w_hbm.at[:, side[j]], w.at[:, side[j]], sems.at[j]) for j in range(3)]
    later = ((wo_hbm, wo), (wi_hbm, wi), (wu_hbm, wu), (cot_hbm.at[seq], cot))
    load_later = [pltpu.make_async_copy(src, dst, sems.at[3 + j]) for j, (src, dst) in enumerate(later)]
    save_k = pltpu.make_async_copy(k_all, k_hbm, sems.at[7])
    save_v = pltpu.make_async_copy(v_all, v_hbm, sems.at[8])

    def save_p(pair):
        slot = lax.rem(pair, 2)
        return pltpu.make_async_copy(p_two.at[slot], p_hbm.at[pl.ds(2 * pair, 2)], p_sems.at[slot])

    @pl.when(step == 0)
    def _():
        for copy in (*load_x[0], load_w[1], load_w[2], *load_x[1], *load_x[2], *load_x[3], load_w[0]):
            copy.start()
        load_w[1].wait()
        load_w[2].wait()

    for j in range(BLOCKS):

        @pl.when(step == j)
        def _(j=j):
            for copy in load_x[j]:
                copy.wait()
            owner = meta_ref[1 + j]
            span = pl.ds(pl.multiple_of(owner * block, block), block)
            wanted = owner * block < length

            @pl.when(wanted)
            def _():
                k_all[span] = nn(xs[j], w[:, side[1]]).astype(bf16)
                v_all[span] = (nn(xs[j], w[:, side[2]]) + vb_ref[...]).astype(bf16)

            @pl.when(jnp.logical_not(wanted))
            def _():
                k_all[span] = jnp.zeros((block, width), bf16)
                v_all[span] = jnp.zeros((block, width), bf16)

    @pl.when(step == BLOCKS - 1)
    def _():
        load_w[0].wait()
        to_log2 = math.log2(math.e) / math.sqrt(HEAD)
        q_ref[...] = ((nn(x_ref[...], w[:, side[0]]) + qb_ref[...]) * to_log2).astype(bf16)
        save_k.start()
        save_v.start()
        for copy in load_later:
            copy.start()

    @pl.when(jnp.logical_and(step >= BLOCKS, step < BLOCKS + pairs))
    def _():
        pair = step - BLOCKS

        @pl.when(pair >= 2)
        def _():
            save_p(pair - 2).wait()

        attend(
            pair, length, q_ref, k_all, v_all, p_two.at[lax.rem(pair, 2)], ctx_ref, linv_ref, acc_ref, top_ref
        )
        save_p(pair).start()

    @pl.when(step == BLOCKS + pairs)
    def _():
        for copy in load_later:
            copy.wait()
        middle_kernel(
            part, chunk, x_ref, ctx_ref, cot, wo, wi, wu, ag_ref, fg_ref, ob_ref, as_ref, ib_ref, ub_ref,
            fs_ref, out_ref, pre_ref, cg_ref, sum_ref, isum_ref, slope_ref,
        )
        for pair in range(max(pairs - 2, 0), pairs):
            save_p(pair).wait()
        save_k.wait()
        save_v.wait()


def front(seq, meta, x, pieces, cot, earlier, weights, vectors):
    _, rows, width = x.shape
    whole_block = len(pieces) == 1
    keys, pairs = (pieces[0].shape[0] if whole_block else BLOCKS * rows), width // PAIR
    block = keys // BLOCKS
    hidden = weights[2].shape[1]
    mine = pl.BlockSpec((None, rows, width), lambda i, m: (seq, 0, 0))
    apart = pl.BlockSpec(memory_space=pl.ANY)

    def whole(t):
        return pl.BlockSpec(t.shape, lambda i, m: (0,) * len(t.shape))

    vectors = [v.reshape(1, -1) for v in vectors]
    operands = [x, *pieces, cot, *weights, *vectors]
    specs = [mine] + [apart] * (len(pieces) + 5) + [whole(v) for v in vectors]
    alias = {}
    if earlier is not None:
        operands.append(earlier)
        specs.append(apart)
        alias = {len(operands): 0}

    def shape(*dims, dtype=bf16):
        return jax.ShapeDtypeStruct(dims, dtype)

    outs = [
        shape(*x.shape), shape(rows, width), shape(keys, width), shape(keys, width),
        shape(2 * pairs, rows, keys), shape(rows, width), shape(pairs, 8, rows, dtype=f32),
        shape(rows, width, dtype=f32), shape(rows, width), shape(8, width, dtype=f32), shape(8, hidden, dtype=f32),
    ]
    out_specs = [mine] + [whole(t) for t in outs[1:]]
    for j in (2, 3, 4):
        out_specs[j] = apart
    return pl.pallas_call(
        functools.partial(front_kernel, min(256, rows), min(768, hidden), seq, whole_block, len(pieces)),
        grid_spec=pltpu.PrefetchScalarGridSpec(
            num_scalar_prefetch=1,
            grid=(BLOCKS + pairs + 1,),
            in_specs=specs,
            out_specs=out_specs,
            scratch_shapes=[
                pltpu.VMEM((BLOCKS, block, width), bf16),
                *[pltpu.VMEM(t.shape, bf16) for t in weights],
                pltpu.VMEM((rows, width), bf16),
                pltpu.VMEM((keys, width), bf16),
                pltpu.VMEM((keys, width), bf16),
                pltpu.VMEM((2, 2, rows, keys), bf16),
                pltpu.VMEM((2, rows, PAIR), f32),
                pltpu.VMEM((2, rows, PAIR), f32),
                pltpu.VMEM((rows, hidden), f32),
                pltpu.SemaphoreType.DMA((13 + 2 * BLOCKS,)),
                pltpu.SemaphoreType.DMA((2,)),
            ],
        ),
        out_shape=outs,
        input_output_aliases=alias,
        compiler_params=pltpu.CompilerParams(vmem_limit_bytes=FRONT_VMEM),
        name="front",
        cost_estimate=pl.CostEstimate(flops=60 << 30, bytes_accessed=60 << 20, transcendentals=0),
    )(meta, *operands)


def back_kernel(
    meta_ref, q_ref, g_ref, ctx_ref, linv_ref, k_ref, v_ref, p_ref, pre_hbm, w_hbm,
    own_ref, near, x_a, x_b, y_a, y_b, far_a, far_b, sum_ref,
    dq_all, dk_all, dv_all, pre, w, staged, acc_ref, dkt_ref, dvt_ref, sems,
):
    step = pl.program_id(0)
    rows, width = pre.shape
    block = near.shape[0]
    half = block // 2
    pairs = width // PAIR
    length = meta_ref[0]
    load_w = pltpu.make_async_copy(w_hbm, w, sems.at[0])
    load_pre = pltpu.make_async_copy(pre_hbm, pre, sems.at[1])
    save = [[pltpu.make_async_copy(staged.at[0], near, sems.at[2])]]
    for j, pair in enumerate(((x_a, x_b), (y_a, y_b), (far_a, far_b)), 1):
        save.append(
            [
                pltpu.make_async_copy(staged.at[j, pl.ds(i * half, half)], pair[i], sems.at[2 + 2 * j + i])
                for i in range(2)
            ]
        )

    @pl.when(step == 0)
    def _():
        load_w.start()
        load_pre.start()

    @pl.when(step < pairs)
    def _():
        attend_back(
            step, length, q_ref, g_ref, ctx_ref, linv_ref, k_ref, v_ref, p_ref,
            dq_all, dk_all, dv_all, acc_ref, dkt_ref, dvt_ref,
        )

    @pl.when(step == pairs)
    def _():
        load_w.wait()
        load_pre.wait()

    for j in range(BLOCKS):

        @pl.when(step == pairs + BLOCKS - 1 - j)
        def _(j=j):
            owner = meta_ref[1 + j]
            span = pl.ds(pl.multiple_of(owner * block, block), block)
            wanted = owner * block < length

            @pl.when(wanted)
            def _():
                terms = nt(dk_all[span], w[:, width : 2 * width]) + nt(dv_all[span], w[:, 2 * width :])
                staged[j] = terms.astype(bf16)

            @pl.when(jnp.logical_not(wanted))
            def _():
                staged[j] = jnp.zeros((block, width), bf16)

            for copy in save[j]:
                copy.start()

    @pl.when(step == pairs + BLOCKS - 1)
    def _():
        dq = dq_all[...]
        own_ref[...] = pre[...] + nt(dq.astype(bf16), w[:, :width])
        sum_ref[0:1] = jnp.sum(dq, 0, keepdims=True)
        for copies in save:
            for copy in copies:
                copy.wait()


def back(meta, queries, grads, context, linv, key_rows, value_rows, weights, pre_one, weight):
    rows, width = queries.shape
    keys = key_rows.shape[0]
    block, pairs = keys // BLOCKS, width // PAIR
    big, _ = sizes(keys)
    last = pairs - 1
    qspec = pl.BlockSpec((rows, PAIR), lambda i, m: (0, jnp.minimum(i, last)))
    kspec = pl.BlockSpec((keys, PAIR), lambda i, m: (0, jnp.minimum(i, last)))
    apart = pl.BlockSpec(memory_space=pl.ANY)

    def whole(*dims):
        return pl.BlockSpec(dims, lambda i, m: (0,) * len(dims))

    return pl.pallas_call(
        back_kernel,
        grid_spec=pltpu.PrefetchScalarGridSpec(
            num_scalar_prefetch=1,
            grid=(pairs + BLOCKS,),
            in_specs=[
                qspec, qspec, qspec, whole(*linv.shape), kspec, kspec,
                pl.BlockSpec((2, rows, keys), lambda i, m: (jnp.minimum(i, last), 0, 0)), apart, apart,
            ],
            out_specs=[whole(rows, width)] + [apart] * 7 + [whole(8, width)],
            scratch_shapes=[
                pltpu.VMEM((rows, width), f32),
                pltpu.VMEM((keys, width), bf16),
                pltpu.VMEM((keys, width), bf16),
                pltpu.VMEM((rows, width), f32),
                pltpu.VMEM(weight.shape, bf16),
                pltpu.VMEM((BLOCKS, block, width), bf16),
                pltpu.VMEM((2, rows, PAIR), f32),
                pltpu.VMEM((PAIR, big), f32),
                pltpu.VMEM((PAIR, big), f32),
                pltpu.SemaphoreType.DMA((2 + 2 * BLOCKS,)),
            ],
        ),
        out_shape=[jax.ShapeDtypeStruct((rows, width), f32)]
        + [jax.ShapeDtypeStruct((block, width), bf16)]
        + [jax.ShapeDtypeStruct((block // 2, width), bf16)] * 6
        + [jax.ShapeDtypeStruct((8, width), f32)],
        compiler_params=pltpu.CompilerParams(vmem_limit_bytes=BACK_VMEM),
        name="back",
        cost_estimate=pl.CostEstimate(flops=45 << 30, bytes_accessed=60 << 20, transcendentals=0),
    )(meta, queries, grads, context, linv, key_rows, value_rows, weights, pre_one, weight)


X_PAIRS = [(0, 1), (1, 0), (2, 3), (3, 2)]
Y_PAIRS = [(0, 2), (2, 0), (1, 3), (3, 1)]


def over_x(block):
    return lax.ppermute(block, "seq", X_PAIRS)


def over_y(block):
    return lax.ppermute(block, "seq", Y_PAIRS)


def sum_all(value):
    sizes_of = [(axis, lax.axis_size(axis)) for axis in ("seq", "dp")]
    if any(size & (size - 1) for _, size in sizes_of):
        return lax.psum(value, ("seq", "dp"))
    for axis, size in sizes_of:
        step = 1
        while step < size:
            value = value + lax.ppermute(value, axis, [(i, i ^ step) for i in range(size)])
            step *= 2
    return value


def fence(values, *others):
    return lax.optimization_barrier((values, *others))[0]


def fence(values, *others):
    return lax.optimization_barrier((values, *others))[0]


def local(
    inputs, cotangent, lengths, triple_weight, output_weight, inner_weight, outer_weight,
    attn_gain, ffn_gain, query_bias, value_bias, output_bias, attn_shift, inner_bias, outer_bias, ffn_shift,
):
    seq_count, tok_count, width = inputs.shape
    half = tok_count // 2
    square = lax.axis_size("seq") == BLOCKS
    weights = (triple_weight, output_weight, inner_weight, outer_weight)
    vectors = (
        query_bias, value_bias, attn_gain, ffn_gain, output_bias, attn_shift, inner_bias, outer_bias, ffn_shift
    )
    places = jnp.arange(BLOCKS, dtype=jnp.int32)
    if square:
        places = lax.axis_index("seq") ^ places
    metas = [jnp.concatenate([lengths[s : s + 1], places]) for s in range(seq_count)]
    def inner(s, *after):
        rows = fence(inputs, *after)[s]
        return over_y(rows[:half]), over_x(rows[half:])

    def outer(s, *after):
        rows = fence(inputs, *after)[s]
        return over_x(rows[:half]), over_y(rows[half:])

    def relay(inside):
        return over_x(inside[0]), over_y(inside[1])

    def second_sums(x_b, y_a, got_x, got_y):
        return (
            (x_b.astype(f32) + got_y.astype(f32)).astype(bf16),
            (y_a.astype(f32) + got_x.astype(f32)).astype(bf16),
        )

    def close(s, own, near, end_x_a, end_y_b, end_x_b, end_y_a):
        total = own + near.astype(f32)
        total = total + jnp.concatenate([end_x_a, end_x_b], 0).astype(f32)
        total = total + jnp.concatenate([end_y_a, end_y_b], 0).astype(f32)
        return lax.dynamic_update_slice(grads_in, total.astype(bf16)[None], (s, 0, 0))

    grads_in = jnp.zeros(inputs.shape, bf16)
    layer_out = None
    bias_parts = []
    pending, ends = None, ()
    turn = ()
    ins, outs, far = {}, {}, {}
    if square:
        ins[0] = inner(0)
        outs[0] = outer(0)
        far[0] = relay(ins[0])
        if seq_count > 1:
            ins[1], outs[1] = inner(1, *far[0]), outer(1, *far[0])
    for s in range(seq_count):
        more, still = s + 1 < seq_count, s + 2 < seq_count
        if square:
            pieces = (inputs, outs[s][0], ins[s][1], ins[s][0], outs[s][1], *far[s])
        else:
            pieces = (lax.all_gather(fence(inputs[s], *turn), "seq", axis=0, tiled=True),)
        layer_out, queries, key_rows, value_rows, kept, context, linv, pre_one, grads, sums, inner_sums = front(
            s, metas[s], inputs, pieces, cotangent, layer_out, weights, vectors
        )
        if square:
            moved = ins[s + 1] if more else ()
            summed = ()
            if pending:
                own, here, end_x_a, x_b, y_a, y_b, got_x, got_y = pending
                summed = (own, here, end_x_a, *second_sums(x_b, y_a, got_x, got_y), y_b)
            grads, moved, summed = lax.optimization_barrier((grads, moved, summed))
            if more:
                ins[s + 1] = moved
                far[s + 1] = relay(moved)
            if still:
                outs[s + 2] = outer(s + 2, grads)
            if pending:
                own, here, end_x_a, x_b, y_a, y_b = summed
                ends = (own, here, end_x_a, over_y(y_b), over_x(x_b), over_y(y_a))
        own, here, *parts, query_sums = back(
            metas[s], queries, grads, context, linv, key_rows, value_rows, kept, pre_one, triple_weight
        )
        bias_parts.append((query_sums, sums, inner_sums))
        if square:
            moved = (ins[s + 1], outs[s + 1], far[s + 1]) if more else ()
            beyond = outs[s + 2] if still else ()
            own, here, parts, moved, beyond, ends = lax.optimization_barrier(
                (own, here, parts, moved, beyond, ends)
            )
            if more:
                ins[s + 1], outs[s + 1], far[s + 1] = moved
            if still:
                outs[s + 2] = beyond
                ins[s + 2] = inner(s + 2, own)
            if ends:
                grads_in = close(s - 1, *ends)
                ends = ()
            x_a, x_b, y_a, y_b, far_a, far_b = parts
            pending = own, here, over_x(x_a), x_b, y_a, y_b, over_x(far_a), over_y(far_b)
        else:
            partial = jnp.concatenate([here, *parts], 0)
            summed = lax.psum_scatter(partial, "seq", scatter_dimension=0, tiled=True)
            grads_in = lax.dynamic_update_slice(
                grads_in, (own + summed.astype(f32)).astype(bf16)[None], (s, 0, 0)
            )
        turn = (own,)
    bias_parts = fence(bias_parts, *turn)
    bias_sums = sum(jnp.concatenate([q[0], t[:5].reshape(-1), n[0]]) for q, t, n in bias_parts)
    if square:
        own, here, end_x_a, x_b, y_a, y_b, got_x, got_y = pending
        end_y_b = over_y(y_b)
        bias_sums, got_x, got_y = lax.optimization_barrier((bias_sums, got_x, got_y))
        x_b, y_a = second_sums(x_b, y_a, got_x, got_y)
        grads_in = close(seq_count - 1, own, here, end_x_a, end_y_b, over_x(x_b), over_y(y_a))
    bias_sums = sum_all(bias_sums)
    query_bias_grad, value_bias_grad, output_bias_grad, attn_shift_grad, outer_bias_grad, ffn_shift_grad = (
        bias_sums[i * width : (i + 1) * width] for i in range(6)
    )
    return (
        layer_out, grads_in, query_bias_grad, value_bias_grad, output_bias_grad,
        attn_shift_grad, bias_sums[6 * width :], outer_bias_grad, ffn_shift_grad,
    )


def solution(mesh):
    split = P("dp", "seq", None)
    return jax.shard_map(
        local,
        mesh=mesh,
        in_specs=(split, split, P("dp")) + (P(),) * 13,
        out_specs=(split, split) + (P(),) * 7,
        check_vma=False,
    )
```

```python
import functools
import math

import jax
import jax.numpy as jnp
from jax import lax
from jax.experimental import pallas as pl
from jax.experimental.pallas import tpu as pltpu
from jax.sharding import PartitionSpec as P

HEAD = 64
PAIR = 128
LOG2_E = math.log2(math.e)
PART = 512
epsilon = 1e-06
NEG = -1e30
SUM_LOW, SUM_HIGH = 2.0**-90, 2.0**100
bf16, f32 = jnp.bfloat16, jnp.float32
FRONT_VMEM, BACK_VMEM = 60 << 20, 56 << 20


def nn(a, b):
    return lax.dot_general(a, b, (((1,), (0,)), ((), ())), preferred_element_type=f32)


def nt(a, b):
    return lax.dot_general(a, b, (((1,), (1,)), ((), ())), preferred_element_type=f32)


def split3(value):
    first = value.astype(bf16).astype(f32)
    second = (value - first).astype(bf16).astype(f32)
    return first, second, value - first - second


def sizes(keys):
    return max(keys // 2, 128), max(keys // 4, 128)


def over_keys(length, keys, step, straight):
    big, small = sizes(keys)
    count = (length + small - 1) // small
    ratio = big // small
    full = count // ratio
    if straight:
        every = count * small >= keys

        @pl.when(every)
        def _():
            step(0, keys)

        full = jnp.where(every, 0, full)
        count = jnp.where(every, 0, count)

    def turn(i, carried):
        step(pl.multiple_of(i * big, big), big)
        return carried

    lax.fori_loop(0, full, turn, 0)
    if ratio > 1:

        @pl.when(count > full * ratio)
        def _():
            step(pl.multiple_of(full * big, small), small)


def pipelined(units, first, second):
    held = None
    for unit in units:
        result = first(unit)
        if held is not None:
            second(*held)
        held = (unit, result)
    second(*held)


def in_head(index, h):
    return (index >= HEAD) == (h == 1)


def attend(pair, length, q_ref, k_ref, v_ref, p_ref, ctx_ref, linv_ref, acc_ref, top_ref):
    rows, keys = q_ref.shape[0], k_ref.shape[0]
    part = min(rows, PART)
    lanes = pl.ds(pl.multiple_of(pair * PAIR, PAIR), PAIR)
    lane = lax.broadcasted_iota(jnp.int32, (rows, PAIR), 1)

    def queries(h, top):
        other = HEAD * (1 - h)
        a, b, c = split3(-top)
        extra = jnp.where(lane == other + 3, 1.0, 0.0)
        for j, piece in enumerate((a, b, c)):
            extra = jnp.where(lane == other + j, piece, extra)
        return jnp.where(in_head(lane, h), q_ref[:, lanes].astype(f32), extra).astype(bf16)

    def key_side(h, start, size):
        other = HEAD * (1 - h)
        at = lax.broadcasted_iota(jnp.int32, (size, PAIR), 1)
        place = start + lax.broadcasted_iota(jnp.int32, (size, PAIR), 0)
        extra = jnp.where(at == other + 3, jnp.where(place < length, 0.0, NEG), 1.0).astype(bf16)
        return jnp.where(in_head(at, h), k_ref[pl.ds(start, size), lanes], extra).T

    def sweep(sides, visit):
        acc_ref[...] = jnp.zeros_like(acc_ref)

        def step(start, size):
            at = lax.broadcasted_iota(jnp.int32, (size, PAIR), 1)
            values = v_ref[pl.ds(start, size), lanes]
            one = jnp.ones((), bf16)
            kt = [key_side(h, start, size) for h in range(2)]
            va = [jnp.where(in_head(at, h), values, one) for h in range(2)]

            def score(unit):
                h, c = unit
                return nn(sides[h][c : c + part], kt[h])

            def weigh(unit, s):
                h, c = unit
                p = jnp.exp2(s * LOG2_E).astype(bf16)
                p_ref[h, c : c + part, pl.ds(start, size)] = p
                acc_ref[h, c : c + part] += nn(p, va[h])

            pipelined([(h, c) for h in range(2) for c in range(0, rows, part)], score, weigh)

        visit(step)

    zero = jnp.zeros((rows, 1), f32)
    plain = [queries(h, zero) for h in range(2)]
    sweep(plain, lambda step: over_keys(length, keys, step, False))

    def sums():
        return jnp.where(lane < HEAD, acc_ref[1], acc_ref[0])

    total = sums()
    fine = jnp.logical_and(jnp.min(total) > SUM_LOW, jnp.max(total) < SUM_HIGH)

    @pl.when(jnp.logical_not(fine))
    def _():
        top_ref[...] = jnp.full_like(top_ref, NEG)
        small = sizes(keys)[1]
        turns = (length + small - 1) // small * (small // PAIR)

        def slowly(step):
            def one(i, carried):
                step(pl.multiple_of(i * PAIR, PAIR), PAIR)
                return carried

            lax.fori_loop(0, turns, one, 0)

        def highest(start, size):
            for h in range(2):
                s = nn(plain[h], key_side(h, start, size))
                top_ref[h] = jnp.maximum(top_ref[h], jnp.max(s, 1, keepdims=True))

        slowly(highest)
        sweep([queries(h, top_ref[h][:, :1]) for h in range(2)], slowly)

    inverse = pltpu.roll(1.0 / sums(), HEAD, 1)
    across = inverse.T
    linv_ref[pair, 0:1] = across[0:1]
    linv_ref[pair, 1:2] = across[HEAD : HEAD + 1]
    ctx_ref[:, lanes] = (jnp.where(lane < HEAD, acc_ref[0], acc_ref[1]) * inverse).astype(bf16)


def attend_back(
    pair, length, q_ref, g_ref, ctx_ref, linv_ref, k_ref, v_ref, p_ref,
    dq_ref, dk_ref, dv_ref, acc_ref, dkt_ref, dvt_ref,
):
    rows, keys = q_ref.shape[0], k_ref.shape[0]
    lanes = pl.ds(pl.multiple_of(pair * PAIR, PAIR), PAIR)
    lane = lax.broadcasted_iota(jnp.int32, (rows, PAIR), 1)
    grad = g_ref[...].astype(f32)
    inverse = jnp.concatenate(
        [jnp.broadcast_to(linv_ref[pair, h : h + 1], (HEAD, rows)) for h in range(2)], 0
    ).T
    product = grad * ctx_ref[...].astype(f32) * inverse
    scaled = grad * inverse
    sides = []
    for h in range(2):
        other = HEAD * (1 - h)
        delta = jnp.sum(jnp.where(in_head(lane, h), product, 0.0), 1, keepdims=True)
        extra = jnp.zeros((rows, PAIR), f32)
        for j, piece in enumerate(split3(-delta)):
            extra = jnp.where(lane == other + j, piece, extra)
        sides.append(jnp.where(in_head(lane, h), scaled, extra).astype(bf16))
    gt = scaled.astype(bf16).T
    qt = q_ref[...].T
    acc_ref[...] = jnp.zeros_like(acc_ref)
    big, small = sizes(keys)
    count = (length + small - 1) // small

    def step(start, size):
        at = lax.broadcasted_iota(jnp.int32, (size, PAIR), 1)
        span = pl.ds(start, size)
        key_rows, value_rows = k_ref[span], v_ref[span]
        one = jnp.ones((), bf16)
        vt = [jnp.where(in_head(at, h), value_rows, one).T for h in range(2)]

        def first(h):
            return nn(sides[h], vt[h])

        def second(h, dp):
            p = p_ref[h, :, span]
            ds = (p.astype(f32) * dp).astype(bf16)
            acc_ref[h] += nn(ds, key_rows)
            mine = slice(HEAD * h, HEAD * h + HEAD)
            dvt_ref[mine, :size] = nn(gt, p)[mine]
            dkt_ref[mine, :size] = nn(qt, ds)[mine]

        pipelined(range(2), first, second)
        dk_ref[span, lanes] = dkt_ref[:, :size].astype(bf16).T
        dv_ref[span, lanes] = dvt_ref[:, :size].astype(bf16).T

    over_keys(length, keys, step, True)

    def blank(i, carried):
        span = pl.ds(pl.multiple_of(i * small, small), small)
        dk_ref[span, lanes] = jnp.zeros((small, PAIR), bf16)
        dv_ref[span, lanes] = jnp.zeros((small, PAIR), bf16)
        return carried

    lax.fori_loop(count, keys // small, blank, 0)
    dq_ref[:, lanes] = jnp.where(lane < HEAD, acc_ref[0], acc_ref[1]) * (1.0 / math.sqrt(HEAD))


def layer_norm(hidden):
    center = hidden - jnp.mean(hidden, -1, keepdims=True)
    inverse = lax.rsqrt(jnp.mean(center * center, -1, keepdims=True) + epsilon)
    return (center * inverse, inverse)


def norm_back(gradient, normed, inverse):
    return (
        gradient
        - jnp.mean(gradient, -1, keepdims=True)
        - normed * jnp.mean(gradient * normed, -1, keepdims=True)
    ) * inverse


def middle_kernel(part, chunk, x_ref, ctx_ref, cot_ref, wo_ref, wi_ref, wu_ref, ag_ref, fg_ref, ob_ref, as_ref, ib_ref, ub_ref, fs_ref,
                  out_ref, pre_ref, cg_ref, sum_ref, isum_ref, slope_ref):
    rows, width = x_ref.shape
    hidden_width = wi_ref.shape[1]
    cuts = [slice(c, c + chunk) for c in range(0, hidden_width, chunk)]
    def colsum(t): return jnp.sum(t, 0, keepdims=True)
    totals = {}
    def add(name, t):
        totals[name] = totals[name] + colsum(t) if name in totals else colsum(t)
    def stages(r):
        span = slice(r, r + part)
        branch = nn(ctx_ref[span], wo_ref[...]) + ob_ref[...]
        normed_one, inverse_one = layer_norm(x_ref[span].astype(f32) + branch)
        mid = normed_one * ag_ref[...] + as_ref[...]
        low = mid.astype(bf16)
        yield
        total = None
        held = None
        def finish(cut, h):
            e = jnp.exp2(h * h * (-0.5 * math.log2(math.e)))
            phi = 0.5 + 0.5 * lax.erf(h * math.sqrt(0.5))
            slope_ref[span, cut] = phi + h * (e * (1.0 / math.sqrt(2.0 * math.pi)))
            return nn((h * phi).astype(bf16), wu_ref[cut])
        for cut in cuts:
            h = nn(low, wi_ref[:, cut]) + ib_ref[:, cut]
            if held is not None:
                t = finish(*held); total = t if total is None else total + t
            held = (cut, h)
        t = finish(*held); total = t if total is None else total + t
        yield
        normed_two, inverse_two = layer_norm(mid + total + ub_ref[...])
        out_ref[span] = (normed_two * fg_ref[...] + fs_ref[...]).astype(bf16)
        cot = cot_ref[span].astype(f32)
        pre_two = norm_back(cot * fg_ref[...], normed_two, inverse_two)
        add("cot", cot); add("two", pre_two)
        low = pre_two.astype(bf16)
        yield
        total = pre_two
        held = None
        def back(cut, d):
            g = d * slope_ref[span, cut]
            add(("inner", cut.start), g)
            return nt(g.astype(bf16), wi_ref[:, cut])
        for cut in cuts:
            d = nt(low, wu_ref[cut])
            if held is not None: total = total + back(*held)
            held = (cut, d)
        total = total + back(*held)
        yield
        add("mid", total)
        pre_one = norm_back(total * ag_ref[...], normed_one, inverse_one)
        add("one", pre_one)
        pre_ref[span] = pre_one
        cg = nt(pre_one.astype(bf16), wo_ref[...])
        add("ctx", cg)
        cg_ref[span] = cg.astype(bf16)
        yield
    flows = [stages(r) for r in range(0, rows, part)]
    n = 5
    for t in range(n + len(flows) - 1):
        for i, f in enumerate(flows):
            if 0 <= t - i < n: next(f)
    for j, name in enumerate(("ctx", "one", "mid", "two", "cot")):
        sum_ref[j:j+1] = totals[name]
    for cut in cuts: isum_ref[0:1, cut] = totals[("inner", cut.start)]

BLOCKS = 4


def front_kernel(part, chunk, seq, whole_block, count, meta_ref, x_ref, *refs):
    pieces, refs = refs[:count], refs[count:]
    (
        cot_hbm, w_hbm, wo_hbm, wi_hbm, wu_hbm,
        qb_ref, vb_ref, ag_ref, fg_ref, ob_ref, as_ref, ib_ref, ub_ref, fs_ref,
    ) = refs[:14]
    (
        out_ref, q_ref, k_hbm, v_hbm, p_hbm, ctx_ref, linv_ref, pre_ref, cg_ref, sum_ref, isum_ref,
        xs, w, wo, wi, wu, cot, k_all, v_all, p_two, acc_ref, top_ref, slope_ref, sems, p_sems,
    ) = refs[-25:]
    step = pl.program_id(0)
    pairs = p_hbm.shape[0] // 2
    block, width = xs.shape[1:]
    length = meta_ref[0]
    side = [slice(j * width, (j + 1) * width) for j in range(3)]
    load_x = []
    for j in range(BLOCKS):
        if whole_block:
            parts = [(pieces[0].at[pl.ds(j * block, block)], xs.at[j])]
        elif j == 0:
            parts = [(pieces[0].at[seq], xs.at[0])]
        else:
            half = block // 2
            parts = [(pieces[2 * j - 1 + i], xs.at[j, pl.ds(i * half, half)]) for i in range(2)]
        load_x.append([pltpu.make_async_copy(src, dst, sems.at[13 + 2 * j + i]) for i, (src, dst) in enumerate(parts)])
    load_w = [pltpu.make_async_copy(w_hbm.at[:, side[j]], w.at[:, side[j]], sems.at[j]) for j in range(3)]
    later = ((wo_hbm, wo), (wi_hbm, wi), (wu_hbm, wu), (cot_hbm.at[seq], cot))
    load_later = [pltpu.make_async_copy(src, dst, sems.at[3 + j]) for j, (src, dst) in enumerate(later)]
    save_k = pltpu.make_async_copy(k_all, k_hbm, sems.at[7])
    save_v = pltpu.make_async_copy(v_all, v_hbm, sems.at[8])

    def save_p(pair):
        slot = lax.rem(pair, 2)
        return pltpu.make_async_copy(p_two.at[slot], p_hbm.at[pl.ds(2 * pair, 2)], p_sems.at[slot])

    @pl.when(step == 0)
    def _():
        for copy in (*load_x[0], load_w[1], load_w[2], *load_x[1], *load_x[2], *load_x[3], load_w[0]):
            copy.start()
        load_w[1].wait()
        load_w[2].wait()

    for j in range(BLOCKS):

        @pl.when(step == j)
        def _(j=j):
            for copy in load_x[j]:
                copy.wait()
            owner = meta_ref[1 + j]
            span = pl.ds(pl.multiple_of(owner * block, block), block)
            wanted = owner * block < length

            @pl.when(wanted)
            def _():
                k_all[span] = nn(xs[j], w[:, side[1]]).astype(bf16)
                v_all[span] = (nn(xs[j], w[:, side[2]]) + vb_ref[...]).astype(bf16)

            @pl.when(jnp.logical_not(wanted))
            def _():
                k_all[span] = jnp.zeros((block, width), bf16)
                v_all[span] = jnp.zeros((block, width), bf16)

    @pl.when(step == BLOCKS - 1)
    def _():
        load_w[0].wait()
        q_ref[...] = ((nn(x_ref[...], w[:, side[0]]) + qb_ref[...]) * (1.0 / math.sqrt(HEAD))).astype(bf16)
        save_k.start()
        save_v.start()
        for copy in load_later:
            copy.start()

    @pl.when(jnp.logical_and(step >= BLOCKS, step < BLOCKS + pairs))
    def _():
        pair = step - BLOCKS

        @pl.when(pair >= 2)
        def _():
            save_p(pair - 2).wait()

        attend(
            pair, length, q_ref, k_all, v_all, p_two.at[lax.rem(pair, 2)], ctx_ref, linv_ref, acc_ref, top_ref
        )
        save_p(pair).start()

    @pl.when(step == BLOCKS + pairs)
    def _():
        for copy in load_later:
            copy.wait()
        middle_kernel(
            part, chunk, x_ref, ctx_ref, cot, wo, wi, wu, ag_ref, fg_ref, ob_ref, as_ref, ib_ref, ub_ref,
            fs_ref, out_ref, pre_ref, cg_ref, sum_ref, isum_ref, slope_ref,
        )
        for pair in range(max(pairs - 2, 0), pairs):
            save_p(pair).wait()
        save_k.wait()
        save_v.wait()


def front(seq, meta, x, pieces, cot, earlier, weights, vectors):
    _, rows, width = x.shape
    whole_block = len(pieces) == 1
    keys, pairs = (pieces[0].shape[0] if whole_block else BLOCKS * rows), width // PAIR
    block = keys // BLOCKS
    hidden = weights[2].shape[1]
    mine = pl.BlockSpec((None, rows, width), lambda i, m: (seq, 0, 0))
    apart = pl.BlockSpec(memory_space=pl.ANY)

    def whole(t):
        return pl.BlockSpec(t.shape, lambda i, m: (0,) * len(t.shape))

    vectors = [v.reshape(1, -1) for v in vectors]
    operands = [x, *pieces, cot, *weights, *vectors]
    specs = [mine] + [apart] * (len(pieces) + 5) + [whole(v) for v in vectors]
    alias = {}
    if earlier is not None:
        operands.append(earlier)
        specs.append(apart)
        alias = {len(operands): 0}

    def shape(*dims, dtype=bf16):
        return jax.ShapeDtypeStruct(dims, dtype)

    outs = [
        shape(*x.shape), shape(rows, width), shape(keys, width), shape(keys, width),
        shape(2 * pairs, rows, keys), shape(rows, width), shape(pairs, 8, rows, dtype=f32),
        shape(rows, width, dtype=f32), shape(rows, width), shape(8, width, dtype=f32), shape(8, hidden, dtype=f32),
    ]
    out_specs = [mine] + [whole(t) for t in outs[1:]]
    for j in (2, 3, 4):
        out_specs[j] = apart
    return pl.pallas_call(
        functools.partial(front_kernel, min(256, rows), min(768, hidden), seq, whole_block, len(pieces)),
        grid_spec=pltpu.PrefetchScalarGridSpec(
            num_scalar_prefetch=1,
            grid=(BLOCKS + pairs + 1,),
            in_specs=specs,
            out_specs=out_specs,
            scratch_shapes=[
                pltpu.VMEM((BLOCKS, block, width), bf16),
                *[pltpu.VMEM(t.shape, bf16) for t in weights],
                pltpu.VMEM((rows, width), bf16),
                pltpu.VMEM((keys, width), bf16),
                pltpu.VMEM((keys, width), bf16),
                pltpu.VMEM((2, 2, rows, keys), bf16),
                pltpu.VMEM((2, rows, PAIR), f32),
                pltpu.VMEM((2, rows, PAIR), f32),
                pltpu.VMEM((rows, hidden), f32),
                pltpu.SemaphoreType.DMA((13 + 2 * BLOCKS,)),
                pltpu.SemaphoreType.DMA((2,)),
            ],
        ),
        out_shape=outs,
        input_output_aliases=alias,
        compiler_params=pltpu.CompilerParams(vmem_limit_bytes=FRONT_VMEM),
        name="front",
        cost_estimate=pl.CostEstimate(flops=60 << 30, bytes_accessed=60 << 20, transcendentals=0),
    )(meta, *operands)


def back_kernel(
    meta_ref, q_ref, g_ref, ctx_ref, linv_ref, k_ref, v_ref, p_ref, pre_hbm, w_hbm, before_ref, row_ref, inner_ref,
    own_ref, near, x_a, x_b, y_a, y_b, far_a, far_b, sum_ref,
    dq_all, dk_all, dv_all, pre, w, staged, acc_ref, dkt_ref, dvt_ref, sems,
):
    step = pl.program_id(0)
    rows, width = pre.shape
    block = near.shape[0]
    half = block // 2
    pairs = width // PAIR
    length = meta_ref[0]
    load_w = pltpu.make_async_copy(w_hbm, w, sems.at[0])
    load_pre = pltpu.make_async_copy(pre_hbm, pre, sems.at[1])
    save = [[pltpu.make_async_copy(staged.at[0], near, sems.at[2])]]
    for j, pair in enumerate(((x_a, x_b), (y_a, y_b), (far_a, far_b)), 1):
        save.append(
            [
                pltpu.make_async_copy(staged.at[j, pl.ds(i * half, half)], pair[i], sems.at[2 + 2 * j + i])
                for i in range(2)
            ]
        )

    @pl.when(step == 0)
    def _():
        load_w.start()
        load_pre.start()

    @pl.when(step < pairs)
    def _():
        attend_back(
            step, length, q_ref, g_ref, ctx_ref, linv_ref, k_ref, v_ref, p_ref,
            dq_all, dk_all, dv_all, acc_ref, dkt_ref, dvt_ref,
        )

    @pl.when(step == pairs)
    def _():
        load_w.wait()
        load_pre.wait()

    for j in range(BLOCKS):

        @pl.when(step == pairs + BLOCKS - 1 - j)
        def _(j=j):
            owner = meta_ref[1 + j]
            span = pl.ds(pl.multiple_of(owner * block, block), block)
            wanted = owner * block < length

            @pl.when(wanted)
            def _():
                terms = nt(dk_all[span], w[:, width : 2 * width]) + nt(dv_all[span], w[:, 2 * width :])
                staged[j] = terms.astype(bf16)

            @pl.when(jnp.logical_not(wanted))
            def _():
                staged[j] = jnp.zeros((block, width), bf16)

            for copy in save[j]:
                copy.start()

    @pl.when(step == pairs + BLOCKS - 1)
    def _():
        dq = dq_all[...]
        own_ref[...] = pre[...] + nt(dq.astype(bf16), w[:, :width])
        sum_ref[...] = before_ref[...]
        sum_ref[0:1] += jnp.sum(dq, 0, keepdims=True)
        sum_ref[1:6] += row_ref[0:5]
        for j in range(inner_ref.shape[1] // width):
            sum_ref[6 + j : 7 + j] += inner_ref[0:1, j * width : (j + 1) * width]
        for copies in save:
            for copy in copies:
                copy.wait()


def back(meta, queries, grads, context, linv, key_rows, value_rows, weights, pre_one, weight, before, sums, inner_sums):
    rows, width = queries.shape
    keys = key_rows.shape[0]
    block, pairs = keys // BLOCKS, width // PAIR
    last = pairs - 1
    qspec = pl.BlockSpec((rows, PAIR), lambda i, m: (0, jnp.minimum(i, last)))
    kspec = pl.BlockSpec((keys, PAIR), lambda i, m: (0, jnp.minimum(i, last)))
    apart = pl.BlockSpec(memory_space=pl.ANY)

    def whole(*dims):
        return pl.BlockSpec(dims, lambda i, m: (0,) * len(dims))

    return pl.pallas_call(
        back_kernel,
        grid_spec=pltpu.PrefetchScalarGridSpec(
            num_scalar_prefetch=1,
            grid=(pairs + BLOCKS,),
            in_specs=[
                qspec, qspec, qspec, whole(*linv.shape), kspec, kspec,
                pl.BlockSpec((2, rows, keys), lambda i, m: (jnp.minimum(i, last), 0, 0)), apart, apart,
                whole(*before.shape), whole(*sums.shape), whole(*inner_sums.shape),
            ],
            out_specs=[whole(rows, width)] + [apart] * 7 + [whole(*before.shape)],
            scratch_shapes=[
                pltpu.VMEM((rows, width), f32),
                pltpu.VMEM((keys, width), bf16),
                pltpu.VMEM((keys, width), bf16),
                pltpu.VMEM((rows, width), f32),
                pltpu.VMEM(weight.shape, bf16),
                pltpu.VMEM((BLOCKS, block, width), bf16),
                pltpu.VMEM((2, rows, PAIR), f32),
                pltpu.VMEM((PAIR, keys), f32),
                pltpu.VMEM((PAIR, keys), f32),
                pltpu.SemaphoreType.DMA((2 + 2 * BLOCKS,)),
            ],
        ),
        out_shape=[jax.ShapeDtypeStruct((rows, width), f32)]
        + [jax.ShapeDtypeStruct((block, width), bf16)]
        + [jax.ShapeDtypeStruct((block // 2, width), bf16)] * 6
        + [jax.ShapeDtypeStruct(before.shape, f32)],
        compiler_params=pltpu.CompilerParams(vmem_limit_bytes=BACK_VMEM),
        name="back",
        cost_estimate=pl.CostEstimate(flops=45 << 30, bytes_accessed=60 << 20, transcendentals=0),
    )(meta, queries, grads, context, linv, key_rows, value_rows, weights, pre_one, weight, before, sums, inner_sums)


X_PAIRS = [(0, 1), (1, 0), (2, 3), (3, 2)]
Y_PAIRS = [(0, 2), (2, 0), (1, 3), (3, 1)]


def over_x(block):
    return lax.ppermute(block, "seq", X_PAIRS)


def over_y(block):
    return lax.ppermute(block, "seq", Y_PAIRS)


def sum_stages():
    stages = []
    for axis in ("seq", "dp"):
        size, step = lax.axis_size(axis), 1
        if size & (size - 1):
            return [lambda value: lax.psum(value, ("seq", "dp"))]
        while step < size:
            route = [(i, i ^ step) for i in range(size)]
            stages.append(lambda value, axis=axis, route=route: value + lax.ppermute(value, axis, route))
            step *= 2
    return stages


def fence(values, *others):
    return lax.optimization_barrier((values, *others))[0]


def fence(values, *others):
    return lax.optimization_barrier((values, *others))[0]


def local(
    inputs, cotangent, lengths, triple_weight, output_weight, inner_weight, outer_weight,
    attn_gain, ffn_gain, query_bias, value_bias, output_bias, attn_shift, inner_bias, outer_bias, ffn_shift,
):
    seq_count, tok_count, width = inputs.shape
    half = tok_count // 2
    square = lax.axis_size("seq") == BLOCKS
    weights = (triple_weight, output_weight, inner_weight, outer_weight)
    vectors = (
        query_bias, value_bias, attn_gain, ffn_gain, output_bias, attn_shift, inner_bias, outer_bias, ffn_shift
    )
    places = jnp.arange(BLOCKS, dtype=jnp.int32)
    if square:
        places = lax.axis_index("seq") ^ places
    metas = [jnp.concatenate([lengths[s : s + 1], places]) for s in range(seq_count)]
    def inner(s, *after):
        rows = fence(inputs, *after)[s]
        return over_y(rows[:half]), over_x(rows[half:])

    def outer(s, *after):
        rows = fence(inputs, *after)[s]
        return over_x(rows[:half]), over_y(rows[half:])

    def relay(inside):
        return over_x(inside[0]), over_y(inside[1])

    def second_sums(x_b, y_a, got_x, got_y):
        return (
            (x_b.astype(f32) + got_y.astype(f32)).astype(bf16),
            (y_a.astype(f32) + got_x.astype(f32)).astype(bf16),
        )

    def close(s, own, near, end_x_a, end_y_b, end_x_b, end_y_a):
        total = own + near.astype(f32)
        total = total + jnp.concatenate([end_x_a, end_x_b], 0).astype(f32)
        total = total + jnp.concatenate([end_y_a, end_y_b], 0).astype(f32)
        return lax.dynamic_update_slice(grads_in, total.astype(bf16)[None], (s, 0, 0))

    grads_in = jnp.zeros(inputs.shape, bf16)
    layer_out = None
    bias_sums = jnp.zeros((16, width), f32)
    pending, ends = None, ()
    turn = ()
    ins, outs, far = {}, {}, {}
    if square:
        ins[0] = inner(0)
        outs[0] = outer(0)
        far[0] = relay(ins[0])
        if seq_count > 1:
            ins[1], outs[1] = inner(1, *outs[0]), outer(1, *outs[0])
    for s in range(seq_count):
        more, still = s + 1 < seq_count, s + 2 < seq_count
        if square:
            pieces = (inputs, outs[s][0], ins[s][1], ins[s][0], outs[s][1], *far[s])
        else:
            pieces = (lax.all_gather(fence(inputs[s], *turn), "seq", axis=0, tiled=True),)
        layer_out, queries, key_rows, value_rows, kept, context, linv, pre_one, grads, sums, inner_sums = front(
            s, metas[s], inputs, pieces, cotangent, layer_out, weights, vectors
        )
        if square:
            moved = ins[s + 1] if more else ()
            summed = ()
            if pending:
                own, here, end_x_a, x_b, y_a, y_b, got_x, got_y = pending
                summed = (own, here, end_x_a, *second_sums(x_b, y_a, got_x, got_y), y_b)
            grads, moved, summed = lax.optimization_barrier((grads, moved, summed))
            if more:
                ins[s + 1] = moved
                far[s + 1] = relay(moved)
            if still:
                outs[s + 2] = outer(s + 2, grads)
            if pending:
                own, here, end_x_a, x_b, y_a, y_b = summed
                ends = (own, here, end_x_a, over_y(y_b), over_x(x_b), over_y(y_a))
        own, here, *parts, bias_sums = back(
            metas[s], queries, grads, context, linv, key_rows, value_rows, kept, pre_one, triple_weight,
            bias_sums, sums, inner_sums,
        )
        if square:
            moved = (ins[s + 1], outs[s + 1], far[s + 1]) if more else ()
            beyond = outs[s + 2] if still else ()
            own, here, parts, moved, beyond, ends = lax.optimization_barrier(
                (own, here, parts, moved, beyond, ends)
            )
            if more:
                ins[s + 1], outs[s + 1], far[s + 1] = moved
            if still:
                outs[s + 2] = beyond
                ins[s + 2] = inner(s + 2, own)
            if ends:
                grads_in = close(s - 1, *ends)
                ends = ()
            x_a, x_b, y_a, y_b, far_a, far_b = parts
            pending = own, here, over_x(x_a), x_b, y_a, y_b, over_x(far_a), over_y(far_b)
        else:
            partial = jnp.concatenate([here, *parts], 0)
            summed = lax.psum_scatter(partial, "seq", scatter_dimension=0, tiled=True)
            grads_in = lax.dynamic_update_slice(
                grads_in, (own + summed.astype(f32)).astype(bf16)[None], (s, 0, 0)
            )
        turn = (own,)
    stages = sum_stages()
    if square:
        own, here, end_x_a, x_b, y_a, y_b, got_x, got_y = pending
        end_y_b = over_y(y_b)
        bias_sums = stages[0](bias_sums)
        bias_sums, got_x, got_y = lax.optimization_barrier((bias_sums, got_x, got_y))
        x_b, y_a = second_sums(x_b, y_a, got_x, got_y)
        grads_in = close(seq_count - 1, own, here, end_x_a, end_y_b, over_x(x_b), over_y(y_a))
        stages = stages[1:]
    for stage in stages:
        bias_sums = stage(bias_sums)
    query_bias_grad, value_bias_grad, output_bias_grad, attn_shift_grad, outer_bias_grad, ffn_shift_grad = (
        bias_sums[i] for i in range(6)
    )
    inner_bias_grad = bias_sums[6 : 6 + inner_bias.shape[0] // width].reshape(-1)
    return (
        layer_out, grads_in, query_bias_grad, value_bias_grad, output_bias_grad,
        attn_shift_grad, inner_bias_grad, outer_bias_grad, ffn_shift_grad,
    )


def solution(mesh):
    split = P("dp", "seq", None)
    return jax.shard_map(
        local,
        mesh=mesh,
        in_specs=(split, split, P("dp")) + (P(),) * 13,
        out_specs=(split, split) + (P(),) * 7,
        check_vma=False,
    )
```

```python
import functools
import math

import jax
import jax.numpy as jnp
from jax import lax
from jax.experimental import pallas as pl
from jax.experimental.pallas import tpu as pltpu
from jax.sharding import PartitionSpec as P

HEAD = 64
PAIR = 128
LOG2_E = math.log2(math.e)
PART = 512
epsilon = 1e-06
NEG = -1e30
SUM_LOW, SUM_HIGH = 2.0**-90, 2.0**100
bf16, f32 = jnp.bfloat16, jnp.float32
FRONT_VMEM, BACK_VMEM = 60 << 20, 56 << 20


def nn(a, b):
    return lax.dot_general(a, b, (((1,), (0,)), ((), ())), preferred_element_type=f32)


def nt(a, b):
    return lax.dot_general(a, b, (((1,), (1,)), ((), ())), preferred_element_type=f32)


def split3(value):
    first = value.astype(bf16).astype(f32)
    second = (value - first).astype(bf16).astype(f32)
    return first, second, value - first - second


def sizes(keys):
    return max(keys // 2, 128), max(keys // 4, 128)


def over_keys(length, keys, step, straight):
    big, small = sizes(keys)
    count = (length + small - 1) // small
    ratio = big // small
    full = count // ratio
    if straight:
        every = count * small >= keys

        @pl.when(every)
        def _():
            step(0, keys)

        full = jnp.where(every, 0, full)
        count = jnp.where(every, 0, count)

    def turn(i, carried):
        step(pl.multiple_of(i * big, big), big)
        return carried

    lax.fori_loop(0, full, turn, 0)
    if ratio > 1:

        @pl.when(count > full * ratio)
        def _():
            step(pl.multiple_of(full * big, small), small)


def pipelined(units, first, second):
    held = None
    for unit in units:
        result = first(unit)
        if held is not None:
            second(*held)
        held = (unit, result)
    second(*held)


def in_head(index, h):
    return (index >= HEAD) == (h == 1)


def attend(pair, length, q_ref, k_ref, v_ref, p_ref, ctx_ref, linv_ref, acc_ref, top_ref):
    rows, keys = q_ref.shape[0], k_ref.shape[0]
    part = min(rows, PART)
    lanes = pl.ds(pl.multiple_of(pair * PAIR, PAIR), PAIR)
    lane = lax.broadcasted_iota(jnp.int32, (rows, PAIR), 1)

    def queries(h, top):
        other = HEAD * (1 - h)
        a, b, c = split3(-top)
        extra = jnp.where(lane == other + 3, 1.0, 0.0)
        for j, piece in enumerate((a, b, c)):
            extra = jnp.where(lane == other + j, piece, extra)
        return jnp.where(in_head(lane, h), q_ref[:, lanes].astype(f32), extra).astype(bf16)

    def key_side(h, start, size):
        other = HEAD * (1 - h)
        at = lax.broadcasted_iota(jnp.int32, (size, PAIR), 1)
        place = start + lax.broadcasted_iota(jnp.int32, (size, PAIR), 0)
        extra = jnp.where(at == other + 3, jnp.where(place < length, 0.0, NEG), 1.0).astype(bf16)
        return jnp.where(in_head(at, h), k_ref[pl.ds(start, size), lanes], extra).T

    def sweep(sides, visit):
        acc_ref[...] = jnp.zeros_like(acc_ref)

        def step(start, size):
            at = lax.broadcasted_iota(jnp.int32, (size, PAIR), 1)
            values = v_ref[pl.ds(start, size), lanes]
            one = jnp.ones((), bf16)
            kt = [key_side(h, start, size) for h in range(2)]
            va = [jnp.where(in_head(at, h), values, one) for h in range(2)]

            def score(unit):
                h, c = unit
                return nn(sides[h][c : c + part], kt[h])

            def weigh(unit, s):
                h, c = unit
                p = jnp.exp2(s * LOG2_E).astype(bf16)
                p_ref[h, c : c + part, pl.ds(start, size)] = p
                acc_ref[h, c : c + part] += nn(p, va[h])

            pipelined([(h, c) for h in range(2) for c in range(0, rows, part)], score, weigh)

        visit(step)

    zero = jnp.zeros((rows, 1), f32)
    plain = [queries(h, zero) for h in range(2)]
    sweep(plain, lambda step: over_keys(length, keys, step, False))

    def sums():
        return jnp.where(lane < HEAD, acc_ref[1], acc_ref[0])

    total = sums()
    fine = jnp.logical_and(jnp.min(total) > SUM_LOW, jnp.max(total) < SUM_HIGH)

    @pl.when(jnp.logical_not(fine))
    def _():
        top_ref[...] = jnp.full_like(top_ref, NEG)
        small = sizes(keys)[1]
        turns = (length + small - 1) // small * (small // PAIR)

        def slowly(step):
            def one(i, carried):
                step(pl.multiple_of(i * PAIR, PAIR), PAIR)
                return carried

            lax.fori_loop(0, turns, one, 0)

        def highest(start, size):
            for h in range(2):
                s = nn(plain[h], key_side(h, start, size))
                top_ref[h] = jnp.maximum(top_ref[h], jnp.max(s, 1, keepdims=True))

        slowly(highest)
        sweep([queries(h, top_ref[h][:, :1]) for h in range(2)], slowly)

    inverse = pltpu.roll(1.0 / sums(), HEAD, 1)
    across = inverse.T
    linv_ref[pair, 0:1] = across[0:1]
    linv_ref[pair, 1:2] = across[HEAD : HEAD + 1]
    ctx_ref[:, lanes] = (jnp.where(lane < HEAD, acc_ref[0], acc_ref[1]) * inverse).astype(bf16)


def attend_back(
    pair, length, q_ref, g_ref, ctx_ref, linv_ref, k_ref, v_ref, p_ref,
    dq_ref, dk_ref, dv_ref, acc_ref, dkt_ref, dvt_ref,
):
    rows, keys = q_ref.shape[0], k_ref.shape[0]
    lanes = pl.ds(pl.multiple_of(pair * PAIR, PAIR), PAIR)
    lane = lax.broadcasted_iota(jnp.int32, (rows, PAIR), 1)
    grad = g_ref[...].astype(f32)
    inverse = jnp.concatenate(
        [jnp.broadcast_to(linv_ref[pair, h : h + 1], (HEAD, rows)) for h in range(2)], 0
    ).T
    product = grad * ctx_ref[...].astype(f32) * inverse
    scaled = grad * inverse
    sides = []
    for h in range(2):
        other = HEAD * (1 - h)
        delta = jnp.sum(jnp.where(in_head(lane, h), product, 0.0), 1, keepdims=True)
        extra = jnp.zeros((rows, PAIR), f32)
        for j, piece in enumerate(split3(-delta)):
            extra = jnp.where(lane == other + j, piece, extra)
        sides.append(jnp.where(in_head(lane, h), scaled, extra).astype(bf16))
    gt = scaled.astype(bf16).T
    qt = q_ref[...].T
    acc_ref[...] = jnp.zeros_like(acc_ref)
    big, small = sizes(keys)
    count = (length + small - 1) // small

    def step(start, size):
        at = lax.broadcasted_iota(jnp.int32, (size, PAIR), 1)
        span = pl.ds(start, size)
        key_rows, value_rows = k_ref[span], v_ref[span]
        one = jnp.ones((), bf16)
        vt = [jnp.where(in_head(at, h), value_rows, one).T for h in range(2)]

        def first(h):
            return nn(sides[h], vt[h])

        def second(h, dp):
            p = p_ref[h, :, span]
            ds = (p.astype(f32) * dp).astype(bf16)
            acc_ref[h] += nn(ds, key_rows)
            mine = slice(HEAD * h, HEAD * h + HEAD)
            dvt_ref[mine, :size] = nn(gt, p)[mine]
            dkt_ref[mine, :size] = nn(qt, ds)[mine]

        pipelined(range(2), first, second)
        dk_ref[span, lanes] = dkt_ref[:, :size].astype(bf16).T
        dv_ref[span, lanes] = dvt_ref[:, :size].astype(bf16).T

    over_keys(length, keys, step, True)

    def blank(i, carried):
        span = pl.ds(pl.multiple_of(i * small, small), small)
        dk_ref[span, lanes] = jnp.zeros((small, PAIR), bf16)
        dv_ref[span, lanes] = jnp.zeros((small, PAIR), bf16)
        return carried

    lax.fori_loop(count, keys // small, blank, 0)
    dq_ref[:, lanes] = jnp.where(lane < HEAD, acc_ref[0], acc_ref[1]) * (1.0 / math.sqrt(HEAD))


def layer_norm(hidden):
    center = hidden - jnp.mean(hidden, -1, keepdims=True)
    inverse = lax.rsqrt(jnp.mean(center * center, -1, keepdims=True) + epsilon)
    return (center * inverse, inverse)


def norm_back(gradient, normed, inverse):
    return (
        gradient
        - jnp.mean(gradient, -1, keepdims=True)
        - normed * jnp.mean(gradient * normed, -1, keepdims=True)
    ) * inverse


def middle_kernel(part, chunk, x_ref, ctx_ref, cot_ref, wo_ref, wi_ref, wu_ref, ag_ref, fg_ref, ob_ref, as_ref, ib_ref, ub_ref, fs_ref,
                  out_ref, pre_ref, cg_ref, sum_ref, isum_ref, slope_ref):
    rows, width = x_ref.shape
    hidden_width = wi_ref.shape[1]
    cuts = [slice(c, c + chunk) for c in range(0, hidden_width, chunk)]
    def colsum(t): return jnp.sum(t, 0, keepdims=True)
    totals = {}
    def add(name, t):
        totals[name] = totals[name] + colsum(t) if name in totals else colsum(t)
    def stages(r):
        span = slice(r, r + part)
        branch = nn(ctx_ref[span], wo_ref[...]) + ob_ref[...]
        normed_one, inverse_one = layer_norm(x_ref[span].astype(f32) + branch)
        mid = normed_one * ag_ref[...] + as_ref[...]
        low = mid.astype(bf16)
        yield
        total = None
        held = None
        def finish(cut, h):
            e = jnp.exp2(h * h * (-0.5 * math.log2(math.e)))
            phi = 0.5 + 0.5 * lax.erf(h * math.sqrt(0.5))
            slope_ref[span, cut] = phi + h * (e * (1.0 / math.sqrt(2.0 * math.pi)))
            return nn((h * phi).astype(bf16), wu_ref[cut])
        for cut in cuts:
            h = nn(low, wi_ref[:, cut]) + ib_ref[:, cut]
            if held is not None:
                t = finish(*held); total = t if total is None else total + t
            held = (cut, h)
        t = finish(*held); total = t if total is None else total + t
        yield
        normed_two, inverse_two = layer_norm(mid + total + ub_ref[...])
        out_ref[span] = (normed_two * fg_ref[...] + fs_ref[...]).astype(bf16)
        cot = cot_ref[span].astype(f32)
        pre_two = norm_back(cot * fg_ref[...], normed_two, inverse_two)
        add("cot", cot); add("two", pre_two)
        low = pre_two.astype(bf16)
        yield
        total = pre_two
        held = None
        def back(cut, d):
            g = d * slope_ref[span, cut]
            add(("inner", cut.start), g)
            return nt(g.astype(bf16), wi_ref[:, cut])
        for cut in cuts:
            d = nt(low, wu_ref[cut])
            if held is not None: total = total + back(*held)
            held = (cut, d)
        total = total + back(*held)
        yield
        add("mid", total)
        pre_one = norm_back(total * ag_ref[...], normed_one, inverse_one)
        add("one", pre_one)
        pre_ref[span] = pre_one
        cg = nt(pre_one.astype(bf16), wo_ref[...])
        add("ctx", cg)
        cg_ref[span] = cg.astype(bf16)
        yield
    flows = [stages(r) for r in range(0, rows, part)]
    n = 5
    for t in range(n + len(flows) - 1):
        for i, f in enumerate(flows):
            if 0 <= t - i < n: next(f)
    for j, name in enumerate(("ctx", "one", "mid", "two", "cot")):
        sum_ref[j:j+1] = totals[name]
    for cut in cuts: isum_ref[0:1, cut] = totals[("inner", cut.start)]

BLOCKS = 4


def front_kernel(part, chunk, seq, whole_block, count, meta_ref, x_ref, *refs):
    pieces, refs = refs[:count], refs[count:]
    (
        cot_hbm, w_hbm, wo_hbm, wi_hbm, wu_hbm,
        qb_ref, vb_ref, ag_ref, fg_ref, ob_ref, as_ref, ib_ref, ub_ref, fs_ref,
    ) = refs[:14]
    (
        out_ref, q_hbm, k_hbm, v_hbm, p_hbm, ctx_hbm, linv_ref, pre_ref, cg_ref, sum_ref, isum_ref,
        xs, w, wo, wi, wu, cot, k_all, v_all, p_two, acc_ref, top_ref, slope_ref, q_ref, ctx_ref, sems, p_sems,
    ) = refs[-27:]
    step = pl.program_id(0)
    pairs = p_hbm.shape[0] // 2
    block, width = xs.shape[1:]
    length = meta_ref[0]
    side = [slice(j * width, (j + 1) * width) for j in range(3)]
    load_x = []
    for j in range(BLOCKS):
        if whole_block:
            parts = [(pieces[0].at[pl.ds(j * block, block)], xs.at[j])]
        elif j == 0:
            parts = [(pieces[0].at[seq], xs.at[0])]
        else:
            half = block // 2
            parts = [(pieces[2 * j - 1 + i], xs.at[j, pl.ds(i * half, half)]) for i in range(2)]
        load_x.append([pltpu.make_async_copy(src, dst, sems.at[13 + 2 * j + i]) for i, (src, dst) in enumerate(parts)])
    load_w = [pltpu.make_async_copy(w_hbm.at[:, side[j]], w.at[:, side[j]], sems.at[j]) for j in range(3)]
    later = ((wo_hbm, wo), (wi_hbm, wi), (wu_hbm, wu), (cot_hbm.at[seq], cot))
    load_later = [pltpu.make_async_copy(src, dst, sems.at[3 + j]) for j, (src, dst) in enumerate(later)]
    save_k = pltpu.make_async_copy(k_all, k_hbm, sems.at[7])
    save_v = pltpu.make_async_copy(v_all, v_hbm, sems.at[8])
    save_q = pltpu.make_async_copy(q_ref, q_hbm, sems.at[9])
    save_ctx = pltpu.make_async_copy(ctx_ref, ctx_hbm, sems.at[10])

    def save_p(pair):
        slot = lax.rem(pair, 2)
        return pltpu.make_async_copy(p_two.at[slot], p_hbm.at[pl.ds(2 * pair, 2)], p_sems.at[slot])

    @pl.when(step == 0)
    def _():
        for copy in (*load_x[0], load_w[1], load_w[2], *load_x[1], *load_x[2], *load_x[3], load_w[0]):
            copy.start()
        load_w[1].wait()
        load_w[2].wait()

    for j in range(BLOCKS):

        @pl.when(step == j)
        def _(j=j):
            for copy in load_x[j]:
                copy.wait()
            owner = meta_ref[1 + j]
            span = pl.ds(pl.multiple_of(owner * block, block), block)
            wanted = owner * block < length

            @pl.when(wanted)
            def _():
                both = nn(xs[j], w[:, width:])
                k_all[span] = both[:, :width].astype(bf16)
                v_all[span] = (both[:, width:] + vb_ref[...]).astype(bf16)

            @pl.when(jnp.logical_not(wanted))
            def _():
                k_all[span] = jnp.zeros((block, width), bf16)
                v_all[span] = jnp.zeros((block, width), bf16)

    @pl.when(step == BLOCKS - 1)
    def _():
        load_w[0].wait()
        q_ref[...] = ((nn(x_ref[...], w[:, side[0]]) + qb_ref[...]) * (1.0 / math.sqrt(HEAD))).astype(bf16)
        save_q.start()
        save_k.start()
        save_v.start()
        for copy in load_later:
            copy.start()

    @pl.when(jnp.logical_and(step >= BLOCKS, step < BLOCKS + pairs))
    def _():
        pair = step - BLOCKS

        @pl.when(pair >= 2)
        def _():
            save_p(pair - 2).wait()

        attend(
            pair, length, q_ref, k_all, v_all, p_two.at[lax.rem(pair, 2)], ctx_ref, linv_ref, acc_ref, top_ref
        )
        save_p(pair).start()

    @pl.when(step == BLOCKS + pairs)
    def _():
        save_ctx.start()
        for copy in load_later:
            copy.wait()
        middle_kernel(
            part, chunk, x_ref, ctx_ref, cot, wo, wi, wu, ag_ref, fg_ref, ob_ref, as_ref, ib_ref, ub_ref,
            fs_ref, out_ref, pre_ref, cg_ref, sum_ref, isum_ref, slope_ref,
        )
        for pair in range(max(pairs - 2, 0), pairs):
            save_p(pair).wait()
        save_k.wait()
        save_v.wait()
        save_q.wait()
        save_ctx.wait()


def front(seq, meta, x, pieces, cot, earlier, weights, vectors):
    _, rows, width = x.shape
    whole_block = len(pieces) == 1
    keys, pairs = (pieces[0].shape[0] if whole_block else BLOCKS * rows), width // PAIR
    block = keys // BLOCKS
    hidden = weights[2].shape[1]
    mine = pl.BlockSpec((None, rows, width), lambda i, m: (seq, 0, 0))
    apart = pl.BlockSpec(memory_space=pl.ANY)

    def whole(t):
        return pl.BlockSpec(t.shape, lambda i, m: (0,) * len(t.shape))

    vectors = [v.reshape(1, -1) for v in vectors]
    operands = [x, *pieces, cot, *weights, *vectors]
    specs = [mine] + [apart] * (len(pieces) + 5) + [whole(v) for v in vectors]
    alias = {}
    if earlier is not None:
        operands.append(earlier)
        specs.append(apart)
        alias = {len(operands): 0}

    def shape(*dims, dtype=bf16):
        return jax.ShapeDtypeStruct(dims, dtype)

    outs = [
        shape(*x.shape), shape(rows, width), shape(keys, width), shape(keys, width),
        shape(2 * pairs, rows, keys), shape(rows, width), shape(pairs, 8, rows, dtype=f32),
        shape(rows, width, dtype=f32), shape(rows, width), shape(8, width, dtype=f32), shape(8, hidden, dtype=f32),
    ]
    out_specs = [mine] + [whole(t) for t in outs[1:]]
    for j in (1, 2, 3, 4, 5):
        out_specs[j] = apart
    return pl.pallas_call(
        functools.partial(front_kernel, min(256, rows), min(768, hidden), seq, whole_block, len(pieces)),
        grid_spec=pltpu.PrefetchScalarGridSpec(
            num_scalar_prefetch=1,
            grid=(BLOCKS + pairs + 1,),
            in_specs=specs,
            out_specs=out_specs,
            scratch_shapes=[
                pltpu.VMEM((BLOCKS, block, width), bf16),
                *[pltpu.VMEM(t.shape, bf16) for t in weights],
                pltpu.VMEM((rows, width), bf16),
                pltpu.VMEM((keys, width), bf16),
                pltpu.VMEM((keys, width), bf16),
                pltpu.VMEM((2, 2, rows, keys), bf16),
                pltpu.VMEM((2, rows, PAIR), f32),
                pltpu.VMEM((2, rows, PAIR), f32),
                pltpu.VMEM((rows, hidden), f32),
                pltpu.VMEM((rows, width), bf16),
                pltpu.VMEM((rows, width), bf16),
                pltpu.SemaphoreType.DMA((13 + 2 * BLOCKS,)),
                pltpu.SemaphoreType.DMA((2,)),
            ],
        ),
        out_shape=outs,
        input_output_aliases=alias,
        compiler_params=pltpu.CompilerParams(vmem_limit_bytes=FRONT_VMEM),
        name="front",
        cost_estimate=pl.CostEstimate(flops=60 << 30, bytes_accessed=60 << 20, transcendentals=0),
    )(meta, *operands)


def back_kernel(
    meta_ref, q_ref, g_ref, ctx_ref, linv_ref, k_ref, v_ref, p_ref, pre_hbm, w_hbm, before_ref, row_ref, inner_ref,
    own_ref, near, x_a, x_b, y_a, y_b, far_a, far_b, sum_ref,
    dq_all, dk_all, dv_all, pre, w, staged, acc_ref, dkt_ref, dvt_ref, sems,
):
    step = pl.program_id(0)
    rows, width = pre.shape
    block = near.shape[0]
    half = block // 2
    pairs = width // PAIR
    length = meta_ref[0]
    load_w = pltpu.make_async_copy(w_hbm, w, sems.at[0])
    load_pre = pltpu.make_async_copy(pre_hbm, pre, sems.at[1])
    save = [[pltpu.make_async_copy(staged.at[0], near, sems.at[2])]]
    for j, pair in enumerate(((x_a, x_b), (y_a, y_b), (far_a, far_b)), 1):
        save.append(
            [
                pltpu.make_async_copy(staged.at[j, pl.ds(i * half, half)], pair[i], sems.at[2 + 2 * j + i])
                for i in range(2)
            ]
        )

    @pl.when(step == 0)
    def _():
        load_w.start()
        load_pre.start()

    @pl.when(step < pairs)
    def _():
        attend_back(
            step, length, q_ref, g_ref, ctx_ref, linv_ref, k_ref, v_ref, p_ref,
            dq_all, dk_all, dv_all, acc_ref, dkt_ref, dvt_ref,
        )

    @pl.when(step == pairs)
    def _():
        load_w.wait()
        load_pre.wait()

    for j in range(BLOCKS):

        @pl.when(step == pairs + BLOCKS - 1 - j)
        def _(j=j):
            owner = meta_ref[1 + j]
            span = pl.ds(pl.multiple_of(owner * block, block), block)
            wanted = owner * block < length

            @pl.when(wanted)
            def _():
                terms = nt(dk_all[span], w[:, width : 2 * width]) + nt(dv_all[span], w[:, 2 * width :])
                staged[j] = terms.astype(bf16)

            @pl.when(jnp.logical_not(wanted))
            def _():
                staged[j] = jnp.zeros((block, width), bf16)

            for copy in save[j]:
                copy.start()

    @pl.when(step == pairs + BLOCKS - 1)
    def _():
        dq = dq_all[...]
        own_ref[...] = pre[...] + nt(dq.astype(bf16), w[:, :width])
        sum_ref[...] = before_ref[...]
        sum_ref[0:1] += jnp.sum(dq, 0, keepdims=True)
        sum_ref[1:6] += row_ref[0:5]
        for j in range(inner_ref.shape[1] // width):
            sum_ref[6 + j : 7 + j] += inner_ref[0:1, j * width : (j + 1) * width]
        for copies in save:
            for copy in copies:
                copy.wait()


def back(meta, queries, grads, context, linv, key_rows, value_rows, weights, pre_one, weight, before, sums, inner_sums):
    rows, width = queries.shape
    keys = key_rows.shape[0]
    block, pairs = keys // BLOCKS, width // PAIR
    last = pairs - 1
    qspec = pl.BlockSpec((rows, PAIR), lambda i, m: (0, jnp.minimum(i, last)))
    kspec = pl.BlockSpec((keys, PAIR), lambda i, m: (0, jnp.minimum(i, last)))
    apart = pl.BlockSpec(memory_space=pl.ANY)

    def whole(*dims):
        return pl.BlockSpec(dims, lambda i, m: (0,) * len(dims))

    return pl.pallas_call(
        back_kernel,
        grid_spec=pltpu.PrefetchScalarGridSpec(
            num_scalar_prefetch=1,
            grid=(pairs + BLOCKS,),
            in_specs=[
                qspec, qspec, qspec, whole(*linv.shape), kspec, kspec,
                pl.BlockSpec((2, rows, keys), lambda i, m: (jnp.minimum(i, last), 0, 0)), apart, apart,
                whole(*before.shape), whole(*sums.shape), whole(*inner_sums.shape),
            ],
            out_specs=[whole(rows, width)] + [apart] * 7 + [whole(*before.shape)],
            scratch_shapes=[
                pltpu.VMEM((rows, width), f32),
                pltpu.VMEM((keys, width), bf16),
                pltpu.VMEM((keys, width), bf16),
                pltpu.VMEM((rows, width), f32),
                pltpu.VMEM(weight.shape, bf16),
                pltpu.VMEM((BLOCKS, block, width), bf16),
                pltpu.VMEM((2, rows, PAIR), f32),
                pltpu.VMEM((PAIR, keys), f32),
                pltpu.VMEM((PAIR, keys), f32),
                pltpu.SemaphoreType.DMA((2 + 2 * BLOCKS,)),
            ],
        ),
        out_shape=[jax.ShapeDtypeStruct((rows, width), f32)]
        + [jax.ShapeDtypeStruct((block, width), bf16)]
        + [jax.ShapeDtypeStruct((block // 2, width), bf16)] * 6
        + [jax.ShapeDtypeStruct(before.shape, f32)],
        compiler_params=pltpu.CompilerParams(vmem_limit_bytes=BACK_VMEM),
        name="back",
        cost_estimate=pl.CostEstimate(flops=45 << 30, bytes_accessed=60 << 20, transcendentals=0),
    )(meta, queries, grads, context, linv, key_rows, value_rows, weights, pre_one, weight, before, sums, inner_sums)


X_PAIRS = [(0, 1), (1, 0), (2, 3), (3, 2)]
Y_PAIRS = [(0, 2), (2, 0), (1, 3), (3, 1)]


def over_x(block):
    return lax.ppermute(block, "seq", X_PAIRS)


def over_y(block):
    return lax.ppermute(block, "seq", Y_PAIRS)


def sum_stages():
    stages = []
    for axis in ("seq", "dp"):
        size, step = lax.axis_size(axis), 1
        if size & (size - 1):
            return [lambda value: lax.psum(value, ("seq", "dp"))]
        while step < size:
            route = [(i, i ^ step) for i in range(size)]
            stages.append(lambda value, axis=axis, route=route: value + lax.ppermute(value, axis, route))
            step *= 2
    return stages


def fence(values, *others):
    return lax.optimization_barrier((values, *others))[0]


def fence(values, *others):
    return lax.optimization_barrier((values, *others))[0]


def local(
    inputs, cotangent, lengths, triple_weight, output_weight, inner_weight, outer_weight,
    attn_gain, ffn_gain, query_bias, value_bias, output_bias, attn_shift, inner_bias, outer_bias, ffn_shift,
):
    seq_count, tok_count, width = inputs.shape
    half = tok_count // 2
    square = lax.axis_size("seq") == BLOCKS
    weights = (triple_weight, output_weight, inner_weight, outer_weight)
    vectors = (
        query_bias, value_bias, attn_gain, ffn_gain, output_bias, attn_shift, inner_bias, outer_bias, ffn_shift
    )
    places = jnp.arange(BLOCKS, dtype=jnp.int32)
    if square:
        places = lax.axis_index("seq") ^ places
    metas = [jnp.concatenate([lengths[s : s + 1], places]) for s in range(seq_count)]
    def inner(s, *after):
        rows = fence(inputs, *after)[s]
        return over_y(rows[:half]), over_x(rows[half:])

    def outer(s, *after):
        rows = fence(inputs, *after)[s]
        return over_x(rows[:half]), over_y(rows[half:])

    def relay(inside):
        return over_x(inside[0]), over_y(inside[1])

    def second_sums(x_b, y_a, got_x, got_y):
        return (
            (x_b.astype(f32) + got_y.astype(f32)).astype(bf16),
            (y_a.astype(f32) + got_x.astype(f32)).astype(bf16),
        )

    def close(s, own, near, end_x_a, end_y_b, end_x_b, end_y_a):
        total = own + near.astype(f32)
        total = total + jnp.concatenate([end_x_a, end_x_b], 0).astype(f32)
        total = total + jnp.concatenate([end_y_a, end_y_b], 0).astype(f32)
        return lax.dynamic_update_slice(grads_in, total.astype(bf16)[None], (s, 0, 0))

    grads_in = jnp.zeros(inputs.shape, bf16)
    layer_out = None
    bias_sums = jnp.zeros((16, width), f32)
    pending, ends = None, ()
    turn = ()
    ins, outs, far = {}, {}, {}
    if square:
        ins[0] = inner(0)
        outs[0] = outer(0)
        far[0] = relay(ins[0])
        if seq_count > 1:
            ins[1], outs[1] = inner(1, *outs[0]), outer(1, *outs[0])
    for s in range(seq_count):
        more, still = s + 1 < seq_count, s + 2 < seq_count
        if square:
            pieces = (inputs, outs[s][0], ins[s][1], ins[s][0], outs[s][1], *far[s])
        else:
            pieces = (lax.all_gather(fence(inputs[s], *turn), "seq", axis=0, tiled=True),)
        layer_out, queries, key_rows, value_rows, kept, context, linv, pre_one, grads, sums, inner_sums = front(
            s, metas[s], inputs, pieces, cotangent, layer_out, weights, vectors
        )
        if square:
            moved = ins[s + 1] if more else ()
            summed = ()
            if pending:
                own, here, end_x_a, x_b, y_a, y_b, got_x, got_y = pending
                summed = (own, here, end_x_a, *second_sums(x_b, y_a, got_x, got_y), y_b)
            grads, moved, summed = lax.optimization_barrier((grads, moved, summed))
            if more:
                ins[s + 1] = moved
                far[s + 1] = relay(moved)
            if still:
                outs[s + 2] = outer(s + 2, grads)
            if pending:
                own, here, end_x_a, x_b, y_a, y_b = summed
                ends = (own, here, end_x_a, over_y(y_b), over_x(x_b), over_y(y_a))
        own, here, *parts, bias_sums = back(
            metas[s], queries, grads, context, linv, key_rows, value_rows, kept, pre_one, triple_weight,
            bias_sums, sums, inner_sums,
        )
        if square:
            moved = (ins[s + 1], outs[s + 1], far[s + 1]) if more else ()
            beyond = outs[s + 2] if still else ()
            own, here, parts, moved, beyond, ends = lax.optimization_barrier(
                (own, here, parts, moved, beyond, ends)
            )
            if more:
                ins[s + 1], outs[s + 1], far[s + 1] = moved
            if still:
                outs[s + 2] = beyond
                ins[s + 2] = inner(s + 2, own)
            if ends:
                grads_in = close(s - 1, *ends)
                ends = ()
            x_a, x_b, y_a, y_b, far_a, far_b = parts
            pending = own, here, over_x(x_a), x_b, y_a, y_b, over_x(far_a), over_y(far_b)
        else:
            partial = jnp.concatenate([here, *parts], 0)
            summed = lax.psum_scatter(partial, "seq", scatter_dimension=0, tiled=True)
            grads_in = lax.dynamic_update_slice(
                grads_in, (own + summed.astype(f32)).astype(bf16)[None], (s, 0, 0)
            )
        turn = (own,)
    stages = sum_stages()
    if square:
        own, here, end_x_a, x_b, y_a, y_b, got_x, got_y = pending
        end_y_b = over_y(y_b)
        bias_sums = stages[0](bias_sums)
        bias_sums, got_x, got_y = lax.optimization_barrier((bias_sums, got_x, got_y))
        x_b, y_a = second_sums(x_b, y_a, got_x, got_y)
        grads_in = close(seq_count - 1, own, here, end_x_a, end_y_b, over_x(x_b), over_y(y_a))
        stages = stages[1:]
    for stage in stages:
        bias_sums = stage(bias_sums)
    query_bias_grad, value_bias_grad, output_bias_grad, attn_shift_grad, outer_bias_grad, ffn_shift_grad = (
        bias_sums[i] for i in range(6)
    )
    inner_bias_grad = bias_sums[6 : 6 + inner_bias.shape[0] // width].reshape(-1)
    return (
        layer_out, grads_in, query_bias_grad, value_bias_grad, output_bias_grad,
        attn_shift_grad, inner_bias_grad, outer_bias_grad, ffn_shift_grad,
    )


def solution(mesh):
    split = P("dp", "seq", None)
    return jax.shard_map(
        local,
        mesh=mesh,
        in_specs=(split, split, P("dp")) + (P(),) * 13,
        out_specs=(split, split) + (P(),) * 7,
        check_vma=False,
    )
```
